256 devices in a mesh: gx: 8 (over y, core), gy: 32 (over x, z).
Axes of the slice: x: 4, y: 4, z: 8, core: 2. Of those that a mesh axis runs over, the one named last changes fastest.
Arguments:
- right_side: float32 [64, 512, 512], P('gx', 'gy'), may hold values from -8 to 8
- inverse_density: float32 [64, 512, 512], P('gx', 'gy'), may hold values from 0.25 to 4
Outputs:
- correction: float32 [64, 512, 512], P('gx', 'gy')
The draws below stay inside these ranges and needn't reach their ends.
All inputs are finite; a program needn't handle non-finite values.
Results may differ from the reference program's by a relative error of at most 0.0003.
Values sent between devices are 32-bit elements; how exact they have to be, the bound alone decides.
A program may use at most 64 MiB of HBM per device.

```python
import math
import jax
import jax.numpy as jnp
from jax import lax

LEVELS = 4
DEGREE = 2
NX = 64
NY = 512
NZ = 512


def level_of(stream_key, extent, pieces, least, high):
    level = 1.0
    for dim, blocks in pieces:
        heights = jax.random.uniform(jax.random.fold_in(jax.random.fold_in(stream_key, 6), dim), (blocks,), jnp.float32, least / len(pieces), high / len(pieces))
        level = level * jnp.repeat(jnp.exp(heights), extent[dim] // blocks).reshape((-1,) + (1,) * (len(extent) - 1 - dim))
    return level


def centred(stream_key, dims, width, reach, cuts=(), kind=jnp.bfloat16):
    factor_of = level_of(stream_key, dims, cuts, -0.22, 0.18) if cuts else 1.0
    result = jax.random.normal(stream_key, dims, jnp.float32) * width * factor_of
    return jnp.minimum(jnp.maximum(result, -reach), reach).astype(kind)


def setup_inputs(seed: int = 0) -> dict:
    streams_of = jax.random.split(jax.random.key(seed), 3)
    return {
        "right_side": centred(streams_of[0], (NX, NY, NZ), 1.0, 8.0, ((0, 8), (1, 32)), jnp.float32),
        "inverse_density": jnp.clip(jnp.exp(math.log(4.0) - 2.7725887 * jax.random.uniform(streams_of[1], (NX, NY, NZ), jnp.float32) ** level_of(streams_of[1], (NX, NY, NZ), ((0, 8), (1, 32)), -0.2, 0.2)), 0.25, 4.0),
    }


theta_mid = 1.25
delta_half = 0.75

def harmonic(first, second):
    return 2.0 * first * second / (first + second)

def face_weights(padded):
    inner = padded[1:-1, 1:-1]
    weight_x = harmonic(padded[:-1, 1:-1], padded[1:, 1:-1])
    weight_y = harmonic(padded[1:-1, :-1], padded[1:-1, 1:])
    weight_z = harmonic(inner[..., :-1], inner[..., 1:])
    return (weight_x, weight_y, weight_z)

def diag_of(weights, scale):
    weight_x, weight_y, weight_z = weights
    along_z = jnp.pad(weight_z, ((0, 0), (0, 0), (0, 1))) + jnp.pad(weight_z, ((0, 0), (0, 0), (1, 0)))
    return (weight_x[1:] + weight_x[:-1] + weight_y[:, 1:] + weight_y[:, :-1] + along_z) * scale

def stencil(padded, weights, scale):
    weight_x, weight_y, weight_z = weights
    inner = padded[1:-1, 1:-1]
    flux_x = weight_x * (padded[1:, 1:-1] - padded[:-1, 1:-1])
    flux_y = weight_y * (padded[1:-1, 1:] - padded[1:-1, :-1])
    flux_z = weight_z * (inner[..., 1:] - inner[..., :-1])
    spread = flux_x[1:] - flux_x[:-1] + flux_y[:, 1:] - flux_y[:, :-1]
    spread = spread + jnp.pad(flux_z, ((0, 0), (0, 0), (0, 1))) - jnp.pad(flux_z, ((0, 0), (0, 0), (1, 0)))
    return -scale * spread

def smooth(field, resid, operate, inv_diag, steps, need_resid):
    sigma = theta_mid / delta_half
    rho_now = 1.0 / sigma
    direction = inv_diag * resid / theta_mid
    for step in range(steps):
        field = field + direction
        if step + 1 < steps or need_resid:
            resid = resid - operate(direction)
        if step + 1 < steps:
            rho_next = 1.0 / (2.0 * sigma - rho_now)
            direction = rho_next * rho_now * direction + 2.0 * rho_next / delta_half * inv_diag * resid
            rho_now = rho_next
    return (field, resid)

def restrict(values):
    nx, ny, nz = values.shape
    return values.reshape(nx // 2, 2, ny // 2, 2, nz // 2, 2).mean(axis=(1, 3, 5))

def prolong(values):
    nx, ny, nz = values.shape
    grown = jnp.broadcast_to(values[:, None, :, None, :, None], (nx, 2, ny, 2, nz, 2))
    return grown.reshape(2 * nx, 2 * ny, 2 * nz)

def dct_matrix(count):
    wave = jnp.arange(count).astype(jnp.float32)[:, None]
    place = jnp.arange(count).astype(jnp.float32)[None, :]
    norms = jnp.where(wave == 0.0, jnp.sqrt(1.0 / count), jnp.sqrt(2.0 / count))
    return (norms * jnp.cos(jnp.pi * wave * (2.0 * place + 1.0) / (2.0 * count))).astype(jnp.float32)

def inverse_table(totals, starts, counts, scale):
    lam = []
    zeros = []
    for total, start, count in zip(totals, starts, counts):
        wave = (start + jnp.arange(count).astype(jnp.int32)).astype(jnp.float32)
        lam.append(2.0 - 2.0 * jnp.cos(jnp.pi * wave / total))
        zeros.append(wave == 0.0)
    lam_all = (lam[0][:, None, None] + lam[1][None, :, None] + lam[2][None, None, :]) * scale
    zero_all = zeros[0][:, None, None] & zeros[1][None, :, None] & zeros[2][None, None, :]
    return jnp.where(zero_all, 0.0, 1.0 / (lam_all + zero_all.astype(jnp.float32)))

def coarse_solve(resid, scale):
    high = lax.Precision.HIGHEST
    nx, ny, nz = resid.shape
    mat_x, mat_y, mat_z = (dct_matrix(nx), dct_matrix(ny), dct_matrix(nz))
    coeffs = jnp.einsum('ai,ijk->ajk', mat_x, resid, precision=high)
    coeffs = jnp.einsum('bj,ajk->abk', mat_y, coeffs, precision=high)
    coeffs = jnp.einsum('ck,abk->abc', mat_z, coeffs, precision=high)
    coeffs = coeffs * inverse_table((nx, ny, nz), (0, 0, 0), (nx, ny, nz), scale)
    coeffs = jnp.einsum('ai,abc->ibc', mat_x, coeffs, precision=high)
    coeffs = jnp.einsum('bj,ibc->ijc', mat_y, coeffs, precision=high)
    return jnp.einsum('ck,ijc->ijk', mat_z, coeffs, precision=high)

def pad_sides(values):
    return jnp.pad(values, ((1, 1), (1, 1), (0, 0)))

def cycle(rhs, coef, level):
    scale = 4.0 ** (-level)
    weights = face_weights(pad_sides(coef))
    inv_diag = 1.0 / diag_of(weights, scale)

    def operate(values):
        return stencil(pad_sides(values), weights, scale)
    field, resid = smooth(jnp.zeros_like(rhs), rhs, operate, inv_diag, DEGREE, True)
    if level + 1 < LEVELS:
        field = field + prolong(cycle(restrict(resid), restrict(coef), level + 1))
    else:
        field = field + coarse_solve(resid, scale)
    resid = rhs - operate(field)
    field, unused = smooth(field, resid, operate, inv_diag, DEGREE, False)
    return field

def reference(right_side, inverse_density):
    return cycle(right_side, inverse_density, 0)
```

```python
import math
import numpy as np
import jax
import jax.numpy as jnp
from jax import lax
from jax.experimental import pallas as pl
from jax.experimental.pallas import tpu as pltpu
from jax.sharding import PartitionSpec as P

MESH = pl.DeviceIdType.MESH
F32 = jnp.float32
THETA = 1.25
DELTA = 0.75
SIGMA = THETA / DELTA
RHO0 = 1.0 / SIGMA
RHO1 = 1.0 / (2.0 * SIGMA - RHO0)
C_FIRST = 1.0 / THETA
C_OLD = RHO1 * RHO0
C_NEW = 2.0 * RHO1 / DELTA
GX, GY = 8, 32
NEIGHBOURS = [(a, b) for a in (-1, 0, 1) for b in (-1, 0, 1) if (a, b) != (0, 0)]
BRICKS = [(a, b) for a in range(GX) for b in (-1, 0, 1) if (a, b) != (0, 0)]
LINE = [(0, b) for b in range(1, GY)]
PEERS = list(
    dict.fromkeys((a % GX, b % GY) for a, b in NEIGHBOURS + BRICKS + LINE)
)


def dct_matrix(count):
    wave = np.arange(count)[:, None].astype(np.float64)
    place = np.arange(count)[None, :].astype(np.float64)
    norms = np.where(wave == 0, math.sqrt(1.0 / count), math.sqrt(2.0 / count))
    return norms * np.cos(np.pi * wave * (2 * place + 1) / (2 * count))


def constants():
    cx, cy, cz = dct_matrix(8), dct_matrix(64), dct_matrix(64)
    forward = np.einsum("ax,cz->xzac", cx, cz).reshape(512, 512)
    turned = np.stack([np.roll(cy, 32 - 2 * g, axis=1) for g in range(GY)])
    window = np.stack([t.T[24:40] for t in turned])
    lam = [2 - 2 * np.cos(np.pi * np.arange(n) / n) for n in (8, 64, 64)]
    total = (lam[1][:, None, None] + lam[0][None, :, None] + lam[2][None, None, :]) * 4.0**-3
    total[0, 0, 0] = 1.0
    table = 1.0 / total
    table[0, 0, 0] = 0.0
    pair = np.zeros((256, 128))
    pair[np.arange(256), np.arange(256) // 2] = 0.125
    grow = np.zeros((128, 256))
    grow[np.arange(256) // 2, np.arange(256)] = 1.0
    rows = np.zeros((72, 16))
    for j in range(24):
        if 2 <= j < 22:
            rows[j, (j + 4) // 2] = 1.0
    for j in range(16):
        rows[24 + j, 2 + j // 2] = 1.0
    for j in range(12):
        rows[40 + j, 6 + j // 2] = 1.0
    for j in range(8):
        rows[56 + j, 2 * j] = 1.0
        rows[56 + j, 2 * j + 1] = 1.0
    for j in range(2):
        rows[64 + j, 4 + 2 * j] = 1.0
        rows[64 + j, 5 + 2 * j] = 1.0
    out = (forward, forward.T, turned, window, table.reshape(64, 512), pair, grow, rows)
    return tuple(np.ascontiguousarray(v, dtype=np.float32) for v in out)


def device(offset):
    gx, gy = lax.axis_index("gx"), lax.axis_index("gy")
    return (lax.rem(gx + (offset[0] % GX), GX), lax.rem(gy + (offset[1] % GY), GY))


def recip(value):
    guess = pl.reciprocal(value, approx=True)
    return guess * (2.0 - value * guess)


def harm(a, b):
    return (a * b) * recip(a + b)


def up(value, axis, step=1):
    return pltpu.roll(value, value.shape[axis] - step, axis)


def down(value, axis, step=1):
    return pltpu.roll(value, step, axis)


def dot(a, b):
    return jnp.dot(a, b, precision=lax.Precision.HIGHEST, preferred_element_type=F32)


def iota(shape, axis):
    return lax.broadcasted_iota(jnp.int32, shape, axis)


def halo_copies(ref, at, size, halo, send, recv):
    copies = []
    for a, b in NEIGHBOURS:
        take, put = [], []
        for side, s0, n, h in zip((a, b), at, size, halo):
            if side == 0:
                take.append((s0, n))
                put.append(s0)
            elif side > 0:
                take.append((s0 + n - h, h))
                put.append(s0 - h)
            else:
                take.append((s0, h))
                put.append(s0 + n)
        (x_from, x_count), (y_from, y_count) = take
        if b == 0:
            ends = [y_from] + list(range(y_from + 4, y_from + y_count, 8)) + [y_from + y_count]
        else:
            ends = [y_from, y_from + y_count]
        for low, high in zip(ends[:-1], ends[1:]):
            k = len(copies)
            copies.append(
                pltpu.make_async_remote_copy(
                    ref.at[pl.ds(x_from, x_count), pl.ds(low, high - low), :],
                    ref.at[pl.ds(put[0], x_count), pl.ds(put[1] + low - y_from, high - low), :],
                    send.at[k],
                    recv.at[k],
                    device_id=device((a, b)),
                    device_id_type=MESH,
                )
            )
    return copies


def start(copies):
    for c in copies:
        c.start()


def arrive(copies):
    for c in copies:
        c.wait_recv()


def sent(copies):
    for c in copies:
        c.wait_send()


def planes_op(v, wx, wy, wz, lo, hi):
    c = v[lo:hi]
    fx = wx[lo - 1 : hi] * (v[lo : hi + 1] - v[lo - 1 : hi])
    fy = wy[lo:hi] * (up(c, 1) - c)
    fz = wz[lo:hi] * (up(c, 2) - c)
    return (fx[1:] - fx[:-1]) + (fy - down(fy, 1)) + (fz - down(fz, 2))


def ring_op(v, wx, wy, wz):
    fx = wx * (jnp.concatenate([v[1:], v[:1]]) - v)
    fy = wy * (up(v, 1) - v)
    fz = wz * (up(v, 2) - v)
    fx = fx - jnp.concatenate([fx[-1:], fx[:-1]])
    return fx + (fy - down(fy, 1)) + (fz - down(fz, 2))


def flat_op(v, wx, wy, wz):
    fx = wx * (up(v, 1, 64) - v)
    fy = wy * (up(v, 0) - v)
    fz = wz * (up(v, 1) - v)
    return (fx - down(fx, 1, 64)) + (fy - down(fy, 0)) + (fz - down(fz, 1))


def kernel(
    r_in, b_in, fwd_in, inv_in, turn_in, wind_in, table_in, pair, grow, rows, out,
    b0, r0, wx0, wy0, wz0, g0, d0, e0, q0, xp0, y0,
    b1, r1, xp1, b2, r2, xp2, e2, m2, b3, r3, m3,
    fwd, inv, turn, wind, table,
    local, halo_s, halo_r, many_s, many_r,
):
    gx, gy = lax.axis_index("gx"), lax.axis_index("gy")
    own = [
        pltpu.make_async_copy(
            src.at[:, pl.ds(4 * j, 4), :],
            dst.at[pl.ds(3, 8), pl.ds(4 + 4 * j, 4), :],
            local.at[k, j],
        )
        for k, (src, dst) in enumerate(((b_in, b0), (r_in, r0)))
        for j in range(4)
    ]
    fixed = [
        pltpu.make_async_copy(fwd_in, fwd, local.at[2, 0]),
        pltpu.make_async_copy(inv_in, inv, local.at[2, 1]),
        pltpu.make_async_copy(turn_in.at[gy], turn, local.at[2, 2]),
        pltpu.make_async_copy(wind_in.at[gy], wind, local.at[2, 3]),
        pltpu.make_async_copy(table_in, table, local.at[3, 0]),
    ]
    start(own + fixed)
    barrier = pltpu.get_barrier_semaphore()
    for p in PEERS:
        pl.semaphore_signal(barrier, inc=1, device_id=device(p), device_id_type=MESH)

    down0 = rows[56:64, :]
    down2 = rows[64:72, :]

    for c in own[:4]:
        c.wait()
    flat = []
    for i in range(4):
        s = b0[3 + 2 * i, 4:20, :] + b0[4 + 2 * i, 4:20, :]
        flat.append(dot(down0, s))
    flat = jnp.concatenate(flat, axis=0)
    flat = jnp.concatenate([dot(flat[:, :256], pair[...]), dot(flat[:, 256:], pair[...])], axis=1)
    for i in range(4):
        b1[3 + i, 4:12, :] = flat[8 * i : 8 * i + 8]
    half = rows[56:60, 0:8]
    for i in range(2):
        s = flat[16 * i : 16 * i + 8] + flat[16 * i + 8 : 16 * i + 16]
        s = dot(dot(half, s), pair[...])
        b2[2 * gx + i, 4:8, :] = s

    for c in own[4:]:
        c.wait()
    pl.semaphore_wait(barrier, len(PEERS))

    b0_out = halo_copies(b0, (3, 4), (8, 16), (3, 3), halo_s.at[0], halo_r.at[0])
    r0_out = halo_copies(r0, (3, 4), (8, 16), (2, 2), halo_s.at[1], halo_r.at[1])
    b1_out = halo_copies(b1, (3, 4), (4, 8), (3, 4), halo_s.at[2], halo_r.at[2])
    r1_out = halo_copies(r1, (3, 4), (4, 8), (2, 2), halo_s.at[3], halo_r.at[3])
    xp0_out = halo_copies(xp0, (3, 4), (8, 16), (2, 2), halo_s.at[4], halo_r.at[4])
    xp1_out = halo_copies(xp1, (3, 4), (4, 8), (3, 3), halo_s.at[5], halo_r.at[5])
    start(b0_out)
    start(r0_out)
    start(b1_out)

    def bricks(ref, k):
        for a, b in BRICKS:
            pltpu.make_async_remote_copy(
                ref.at[pl.ds(2 * gx, 2), pl.ds(4, 4), :],
                ref.at[pl.ds(2 * gx, 2), pl.ds(4 - 4 * b, 4), :],
                many_s.at[k],
                many_r.at[k],
                device_id=device((a, b)),
                device_id_type=MESH,
            ).start()

    def lines(ref, k):
        for _, b in LINE:
            pltpu.make_async_remote_copy(
                ref.at[pl.ds(32, 2), :],
                ref.at[pl.ds((32 - 2 * b) % 64, 2), :],
                many_s.at[k],
                many_r.at[k],
                device_id=device((0, b)),
                device_id_type=MESH,
            ).start()

    def all_of(ref, k):
        return pltpu.make_async_remote_copy(
            ref, ref, many_s.at[k], many_r.at[k], device_id=device((0, 1)), device_id_type=MESH
        )

    bricks(b2, 0)
    arrive(b0_out)
    arrive(r0_out)

    row = iota((24, 512), 0)
    lane = iota((24, 512), 1)
    edge = jnp.where(gy == GY - 1, 19, jnp.where(gy == 0, 3, -1))
    mul_y = jnp.where(row == edge, 0.0, 2.0)
    mul_z = jnp.where(lane == 511, 0.0, 2.0)
    cut0 = jnp.where(gx == GX - 1, 10, jnp.where(gx == 0, 2, -1))

    wx0[0] = 2.0 * harm(b0[0], b0[1])

    @pl.loop(1, 13)
    def _(i):
        c = b0[i]
        wx = harm(c, b0[i + 1]) * jnp.where(i == cut0, 0.0, 2.0)
        wy = harm(c, up(c, 0)) * mul_y
        wz = harm(c, up(c, 1)) * mul_z
        wx0[i] = wx
        wy0[i] = wy
        wz0[i] = wz
        g = recip((wx + wx0[i - 1]) + (wy + down(wy, 0)) + (wz + down(wz, 1)))
        g0[i] = g
        d0[i] = g * r0[i] * C_FIRST

    def op0(ref, i):
        c = ref[i]
        fy = wy0[i] * (up(c, 0) - c)
        fz = wz0[i] * (up(c, 1) - c)
        fx = wx0[i] * (ref[i + 1] - c) - wx0[i - 1] * (c - ref[i - 1])
        return fx + (fy - down(fy, 0)) + (fz - down(fz, 1))

    @pl.loop(2, 12)
    def _(i):
        q = r0[i] + op0(d0, i)
        q0[i] = q
        e0[i] = C_OLD * d0[i] + C_NEW * (g0[i] * q)

    @pl.loop(3, 11)
    def _(i):
        q = q0[i] + op0(e0, i)
        q0[i] = q
        x = d0[i] + e0[i]
        xp0[i, 4:20, :] = x[4:20]

    flat = []
    for i in range(4):
        s = q0[3 + 2 * i, 4:20, :] + q0[4 + 2 * i, 4:20, :]
        flat.append(dot(down0, s))
    flat = jnp.concatenate(flat, axis=0)
    flat = jnp.concatenate([dot(flat[:, :256], pair[...]), dot(flat[:, 256:], pair[...])], axis=1)
    for i in range(4):
        r1[3 + i, 4:12, :] = flat[8 * i : 8 * i + 8]
    start(r1_out)
    start(xp0_out)

    arrive(b1_out)
    v = b1[...]
    shape = (10, 16, 256)
    edge = jnp.where(gy == GY - 1, 11, jnp.where(gy == 0, 3, -1))
    cut = jnp.where(gx == GX - 1, 6, jnp.where(gx == 0, 2, -1))
    keep_x = jnp.where(iota((9, 16, 256), 0) == cut, 0.0, 0.5)
    wx1 = harm(v[:-1], v[1:]) * keep_x
    wy1 = harm(v, up(v, 1)) * jnp.where(iota(shape, 1) == edge, 0.0, 0.5)
    wz1 = harm(v, up(v, 2)) * jnp.where(iota(shape, 2) == 255, 0.0, 0.5)
    c = slice(1, 9)
    g1 = recip(
        (wx1[1:] + wx1[:-1]) + (wy1[c] + down(wy1[c], 1)) + (wz1[c] + down(wz1[c], 2))
    )

    all_of(m2, 0).wait_recv()

    def to_flat(value):
        value = jnp.where(iota((16, 16, 128), 1) < 8, value, 0.0)
        parts = []
        for t in range(4):
            s = jnp.concatenate(
                [value[4 * t] + value[4 * t + 1], value[4 * t + 2] + value[4 * t + 3]], axis=1
            )
            parts.append(dot(s, pair[...]))
        return dot(down2, jnp.concatenate(parts, axis=1))[0:2]

    v = b2[...]
    b3[32:34, :] = to_flat(v)
    lines(b3, 2)
    shape = (16, 16, 128)
    edge = jnp.where(gy == GY - 1, 7, jnp.where(gy == 0, 3, -1))
    scale = 2.0 * 4.0**-2
    wx2 = harm(v, jnp.concatenate([v[1:], v[:1]])) * jnp.where(iota(shape, 0) == 15, 0.0, scale)
    wy2 = harm(v, up(v, 1)) * jnp.where(iota(shape, 1) == edge, 0.0, scale)
    wz2 = harm(v, up(v, 2)) * jnp.where(iota(shape, 2) == 127, 0.0, scale)
    g2 = recip(
        (wx2 + jnp.concatenate([wx2[-1:], wx2[:-1]]))
        + (wy2 + down(wy2, 1))
        + (wz2 + down(wz2, 2))
    )

    arrive(r1_out)
    f1 = r1[...]
    d = g1 * f1[1:9] * C_FIRST
    q = f1[2:8] + planes_op(d, wx1[1:8], wy1[1:9], wz1[1:9], 1, 7)
    e = C_OLD * d[1:7] + C_NEW * (g1[1:7] * q)
    q = q[1:5] + planes_op(e, wx1[2:7], wy1[2:8], wz1[2:8], 1, 5)
    xp1[3:7, 4:12, :] = (d[2:6] + e[1:5])[:, 4:12, :]
    for i in range(2):
        s = (q[2 * i] + q[2 * i + 1])[4:12]
        s = dot(dot(half, s), pair[...])
        r2[2 * gx + i, 4:8, :] = s
    bricks(r2, 1)
    start(xp1_out)

    all_of(m3, 2).wait_recv()
    v = b3[...]
    shape = (64, 512)
    scale = 2.0 * 4.0**-3
    lane = iota(shape, 1)
    edge = lax.rem(95 - 2 * gy, 64)
    wx3 = harm(v, up(v, 1, 64)) * jnp.where(lane >= 448, 0.0, scale)
    wy3 = harm(v, up(v, 0)) * jnp.where(iota(shape, 0) == edge, 0.0, scale)
    wz3 = harm(v, up(v, 1)) * jnp.where(lax.rem(lane, 64) == 63, 0.0, scale)
    g3 = recip((wx3 + down(wx3, 1, 64)) + (wy3 + down(wy3, 0)) + (wz3 + down(wz3, 1)))

    all_of(m2, 1).wait_recv()
    f2 = r2[...]
    d = g2 * f2 * C_FIRST
    q = f2 + ring_op(d, wx2, wy2, wz2)
    e = C_OLD * d + C_NEW * (g2 * q)
    q = q + ring_op(e, wx2, wy2, wz2)
    xp2[:, 4:8, :] = (d + e)[:, 4:8, :]
    q = jnp.where(iota((16, 16, 128), 1) >= 4, q, 0.0)
    r3[32:34, :] = to_flat(q)
    lines(r3, 3)
    xp2_out = [
        pltpu.make_async_remote_copy(
            xp2.at[:, pl.ds(4, 4), :],
            xp2.at[:, pl.ds(4 - 4 * b, 4), :],
            halo_s.at[6, k],
            halo_r.at[6, k],
            device_id=device((0, b)),
            device_id_type=MESH,
        )
        for k, b in enumerate((-1, 1))
    ]
    start(xp2_out)

    for c in fixed:
        c.wait()
    all_of(m3, 3).wait_recv()
    f3 = r3[...]
    d = g3 * f3 * C_FIRST
    q = f3 + flat_op(d, wx3, wy3, wz3)
    e = C_OLD * d + C_NEW * (g3 * q)
    q = q + flat_op(e, wx3, wy3, wz3)
    t = dot(dot(turn[...], q), fwd[...]) * table[...]
    t = dot(dot(wind[...], t), inv[...])
    w = slice(24, 40)
    x = d[w] + e[w] + t
    w3 = (wx3[w], wy3[w], wz3[w])
    q = f3[w] + flat_op(x, *w3)
    d = g3[w] * q * C_FIRST
    q = q + flat_op(d, *w3)
    x = x + d + (C_OLD * d + C_NEW * (g3[w] * q))

    x = dot(rows[40:56, :], x)
    wide = [dot(x[:, 128 * t : 128 * t + 128], grow[...]) for t in range(4)]
    wide = jnp.stack([wide[i // 4][:, 128 * (i // 2 % 2) : 128 * (i // 2 % 2) + 128] for i in range(16)])
    arrive(xp2_out)
    x = xp2[...] + wide
    q = f2 + ring_op(x, wx2, wy2, wz2)
    d = g2 * q * C_FIRST
    q = q + ring_op(d, wx2, wy2, wz2)
    x = x + d + (C_OLD * d + C_NEW * (g2 * q))
    line = iota((16, 16, 128), 1)
    x = jnp.where((line >= 2) & (line < 10), x, 0.0)
    e2[2:18] = x
    e2[0:2] = x[14:16]
    e2[18:20] = x[0:2]

    wide = [dot(rows[24:40, :], dot(e2[2 * gx + i], grow[...])) for i in range(6)]
    wide = jnp.stack([wide[(i + 1) // 2] for i in range(10)])
    arrive(xp1_out)
    x = xp1[...] + wide
    q = f1[1:9] + planes_op(x, wx1, wy1, wz1, 1, 9)
    d = g1 * q * C_FIRST
    q = q[1:7] + planes_op(d, wx1[1:8], wy1[1:9], wz1[1:9], 1, 7)
    x = x[2:8] + d[1:7] + (C_OLD * d[1:7] + C_NEW * (g1[1:7] * q))
    line = iota((6, 16, 256), 1)
    x = jnp.where((line >= 3) & (line < 13), x, 0.0)

    for i in range(6):
        s = dot(rows[0:24, :], x[i])
        y0[i] = jnp.concatenate([dot(s[:, :128], grow[...]), dot(s[:, 128:], grow[...])], axis=1)
    arrive(xp0_out)

    @pl.loop(1, 13)
    def _(i):
        e0[i] = xp0[i] + y0[(i + 3) // 2 - 2]

    @pl.loop(2, 12)
    def _(i):
        q = r0[i] + op0(e0, i)
        q0[i] = q
        d0[i] = g0[i] * q * C_FIRST

    @pl.loop(3, 11)
    def _(i):
        q = q0[i] + op0(d0, i)
        d = d0[i]
        x = e0[i] + d + (C_OLD * d + C_NEW * (g0[i] * q))
        out[i - 3] = x[4:20]

    sent(b0_out + r0_out + b1_out + r1_out + xp0_out + xp1_out + xp2_out)
    all_of(m2, 0).wait_send()
    all_of(m2, 1).wait_send()
    all_of(m3, 2).wait_send()
    all_of(m3, 3).wait_send()


def local(right_side, inverse_density):
    consts = constants()
    any_spec = pl.BlockSpec(memory_space=pl.ANY)
    vmem_spec = pl.BlockSpec(memory_space=pltpu.VMEM)
    fine = pltpu.VMEM((14, 24, 512), F32)
    scratch = [fine] * 10 + [
        pltpu.VMEM((6, 24, 512), F32),
        pltpu.VMEM((10, 16, 256), F32),
        pltpu.VMEM((10, 16, 256), F32),
        pltpu.VMEM((10, 16, 256), F32),
        pltpu.VMEM((16, 16, 128), F32),
        pltpu.VMEM((16, 16, 128), F32),
        pltpu.VMEM((16, 16, 128), F32),
        pltpu.VMEM((20, 16, 128), F32),
        pltpu.VMEM((len(BRICKS), 8, 128), F32),
        pltpu.VMEM((64, 512), F32),
        pltpu.VMEM((64, 512), F32),
        pltpu.VMEM((len(LINE), 8, 128), F32),
        pltpu.VMEM((512, 512), F32),
        pltpu.VMEM((512, 512), F32),
        pltpu.VMEM((64, 64), F32),
        pltpu.VMEM((16, 64), F32),
        pltpu.VMEM((64, 512), F32),
        pltpu.SemaphoreType.DMA((4, 4)),
        pltpu.SemaphoreType.DMA((7, 12)),
        pltpu.SemaphoreType.DMA((7, 12)),
        pltpu.SemaphoreType.DMA((4,)),
        pltpu.SemaphoreType.DMA((4,)),
    ]
    return pl.pallas_call(
        kernel,
        out_shape=jax.ShapeDtypeStruct((8, 16, 512), F32),
        in_specs=[any_spec] * 7 + [vmem_spec] * 3,
        out_specs=vmem_spec,
        scratch_shapes=scratch,
        compiler_params=pltpu.CompilerParams(
            collective_id=0, has_side_effects=True, vmem_limit_bytes=48 * 2**20
        ),
    )(right_side, inverse_density, *consts)


def solution(mesh):
    return jax.shard_map(
        local,
        mesh=mesh,
        in_specs=(P("gx", "gy", None), P("gx", "gy", None)),
        out_specs=P("gx", "gy", None),
        check_vma=False,
    )
```

```python
import math
import numpy as np
import jax
import jax.numpy as jnp
from jax import lax
from jax.experimental import pallas as pl
from jax.experimental.pallas import tpu as pltpu
from jax.sharding import PartitionSpec as P

MESH = pl.DeviceIdType.MESH
F32 = jnp.float32
THETA = 1.25
DELTA = 0.75
SIGMA = THETA / DELTA
RHO0 = 1.0 / SIGMA
RHO1 = 1.0 / (2.0 * SIGMA - RHO0)
C_FIRST = 1.0 / THETA
C_OLD = RHO1 * RHO0
C_NEW = 2.0 * RHO1 / DELTA
GX, GY = 8, 32
UNROLL = 2
NEIGHBOURS = [(a, b) for a in (-1, 0, 1) for b in (-1, 0, 1) if (a, b) != (0, 0)]
BRICKS = [(a, b) for a in range(GX) for b in (-1, 0, 1) if (a, b) != (0, 0)]
LINE = [(0, b) for b in range(1, GY)]
PEERS = list(
    dict.fromkeys((a % GX, b % GY) for a, b in NEIGHBOURS + BRICKS + LINE)
)


def dct_matrix(count):
    wave = np.arange(count)[:, None].astype(np.float64)
    place = np.arange(count)[None, :].astype(np.float64)
    norms = np.where(wave == 0, math.sqrt(1.0 / count), math.sqrt(2.0 / count))
    return norms * np.cos(np.pi * wave * (2 * place + 1) / (2 * count))


def constants():
    cy, cz = dct_matrix(64), dct_matrix(64)
    along = np.kron(np.eye(2), cz.T)
    turned = np.stack([np.roll(cy, 32 - 2 * g, axis=1) for g in range(GY)])
    window = np.stack([np.pad(t.T[24:40], ((0, 0), (0, 64))) for t in turned])
    turned = np.pad(turned, ((0, 0), (0, 0), (0, 64)))
    lam = [2 - 2 * np.cos(np.pi * np.arange(n) / n) for n in (8, 64, 64)]
    total = (lam[1][:, None, None] + lam[0][None, :, None] + lam[2][None, None, :]) * 4.0**-3
    total[0, 0, 0] = 1.0
    table = 1.0 / total
    table[0, 0, 0] = 0.0
    pair = np.zeros((256, 128))
    pair[np.arange(256), np.arange(256) // 2] = 0.125
    grow = np.zeros((128, 256))
    grow[np.arange(256) // 2, np.arange(256)] = 1.0
    cx = dct_matrix(8)
    cross = np.zeros((2, 2, 4, 4, 128))
    for i in range(4):
        for j in range(4):
            for k, c in enumerate((cx, cx.T)):
                cross[k, 0, i, j] = np.repeat([c[2 * i, 2 * j], c[2 * i + 1, 2 * j + 1]], 64)
                cross[k, 1, i, j] = np.repeat([c[2 * i, 2 * j + 1], c[2 * i + 1, 2 * j]], 64)
    out = (along, along.T, turned, window, table.reshape(64, 512), cross.reshape(64, 128))
    out = tuple(np.ascontiguousarray(v, dtype=np.float32) for v in out)
    return out + (pair.astype(jnp.bfloat16), grow.astype(jnp.bfloat16))


def device(offset):
    gx, gy = lax.axis_index("gx"), lax.axis_index("gy")
    return (lax.rem(gx + (offset[0] % GX), GX), lax.rem(gy + (offset[1] % GY), GY))


def recip(value):
    guess = pl.reciprocal(value, approx=True)
    return guess * (2.0 - value * guess)


def harm(a, b):
    return (a * b) * recip(a + b)


def up(value, axis, step=1):
    return pltpu.roll(value, value.shape[axis] - step, axis)


def down(value, axis, step=1):
    return pltpu.roll(value, step, axis)


def parts(value):
    high = value.astype(jnp.bfloat16)
    return high, (value - high.astype(F32)).astype(jnp.bfloat16)


def pick(value, matrix):
    high, low = parts(value)
    return jnp.dot(high, matrix, preferred_element_type=F32) + jnp.dot(
        low, matrix, preferred_element_type=F32
    )


def halve(ref, base, value):
    tiles = []
    for t in range(value.shape[-1] // 128):
        ref[base + t, 0 : value.shape[0], :] = value[:, 128 * t : 128 * t + 128]
        count = value.shape[0] // 2
        tiles.append(
            ref[base + t, pl.ds(0, count, stride=2), :] + ref[base + t, pl.ds(1, count, stride=2), :]
        )
    return tiles


def double(ref, base, value, low, count):
    n = value.shape[0]
    tiles = []
    for t in range(value.shape[-1] // 128):
        v = value[:, 128 * t : 128 * t + 128]
        ref[base + t, pl.ds(4, n, stride=2), :] = v
        ref[base + t, pl.ds(5, n, stride=2), :] = v
        tiles.append(ref[base + t, low : low + count, :])
    return jnp.concatenate(tiles, axis=1)


def cross_x(value, cross, k):
    v = [value[:, 128 * t : 128 * t + 128] for t in range(4)]
    w = [pltpu.roll(t, 64, 1) for t in v]
    out = []
    for i in range(4):
        acc = None
        for j in range(4):
            row = 32 * k + 4 * i + j
            term = v[j] * cross[row : row + 1, :] + w[j] * cross[row + 16 : row + 17, :]
            acc = term if acc is None else acc + term
        out.append(acc)
    return out


def dot(a, b):
    return jnp.dot(a, b, precision=lax.Precision.HIGHEST, preferred_element_type=F32)


def iota(shape, axis):
    return lax.broadcasted_iota(jnp.int32, shape, axis)


def halo_copies(ref, at, size, halo, send, recv):
    copies = []
    for a, b in NEIGHBOURS:
        take, put = [], []
        for side, s0, n, h in zip((a, b), at, size, halo):
            if side == 0:
                take.append((s0, n))
                put.append(s0)
            elif side > 0:
                take.append((s0 + n - h, h))
                put.append(s0 - h)
            else:
                take.append((s0, h))
                put.append(s0 + n)
        (x_from, x_count), (y_from, y_count) = take
        if b == 0:
            ends = [y_from] + list(range(y_from + 4, y_from + y_count, 8)) + [y_from + y_count]
        else:
            ends = [y_from, y_from + y_count]
        for low, high in zip(ends[:-1], ends[1:]):
            k = len(copies)
            copies.append(
                pltpu.make_async_remote_copy(
                    ref.at[pl.ds(x_from, x_count), pl.ds(low, high - low), :],
                    ref.at[pl.ds(put[0], x_count), pl.ds(put[1] + low - y_from, high - low), :],
                    send.at[k],
                    recv.at[k],
                    device_id=device((a, b)),
                    device_id_type=MESH,
                )
            )
    return copies


def brick_copies(src, dst, side, h, send, recv):
    copies = []
    for k, (a, b) in enumerate(NEIGHBOURS):
        x = {0: pl.ds(0, 8), 1: pl.ds(8 - h, h), -1: pl.ds(0, h)}[a]
        y = {0: pl.ds(0, 16), 1: pl.ds(16 - h, h), -1: pl.ds(0, h)}[b]
        if b == 0:
            to = side.at[pl.ds(0 if a > 0 else h, h), :, :]
        else:
            put_x = {0: pl.ds(3, 8), 1: pl.ds(3 - h, h), -1: pl.ds(11, h)}[a]
            put_y = {1: pl.ds(4 - h, h), -1: pl.ds(20, h)}[b]
            to = dst.at[put_x, put_y, :]
        copies.append(
            pltpu.make_async_remote_copy(
                src.at[x, y, :],
                to,
                send.at[k],
                recv.at[k],
                device_id=device((a, b)),
                device_id_type=MESH,
            )
        )
    return copies


def start(copies):
    for c in copies:
        c.start()


def arrive(copies):
    for c in copies:
        c.wait_recv()


def sent(copies):
    for c in copies:
        c.wait_send()


def planes_op(v, wx, wy, wz, lo, hi):
    c = v[lo:hi]
    fx = wx[lo - 1 : hi] * (v[lo : hi + 1] - v[lo - 1 : hi])
    fy = wy[lo:hi] * (up(c, 1) - c)
    fz = wz[lo:hi] * (up(c, 2) - c)
    return (fx[1:] - fx[:-1]) + (fy - down(fy, 1)) + (fz - down(fz, 2))


def ring_op(v, wx, wy, wz):
    fx = wx * (jnp.concatenate([v[1:], v[:1]]) - v)
    fy = wy * (up(v, 1) - v)
    fz = wz * (up(v, 2) - v)
    fx = fx - jnp.concatenate([fx[-1:], fx[:-1]])
    return fx + (fy - down(fy, 1)) + (fz - down(fz, 2))


def flat_op(v, wx, wy, wz):
    fx = wx * (up(v, 1, 64) - v)
    fy = wy * (up(v, 0) - v)
    fz = wz * (up(v, 1) - v)
    return (fx - down(fx, 1, 64)) + (fy - down(fy, 0)) + (fz - down(fz, 1))


def kernel(
    r_in, b_in, fwd_in, inv_in, turn_in, wind_in, table_in, cross_in, pair_in, grow_in, out,
    bs, rs, xb, xr, b0, r0, wx0, wy0, wz0, g0, d0, e0, q0, xp0, y0, thin,
    b1, r1, xp1, b2, r2, xp2, e2, m2, b3, r3, m3,
    fwd, inv, turn, wind, table, cross, pair, grow,
    local, halo_s, halo_r, many_s, many_r,
):
    gx, gy = lax.axis_index("gx"), lax.axis_index("gy")
    own = [
        pltpu.make_async_copy(b_in, bs, local.at[0, 0]),
        pltpu.make_async_copy(r_in, rs, local.at[0, 1]),
    ]
    small = [
        pltpu.make_async_copy(pair_in, pair, local.at[3, 2]),
        pltpu.make_async_copy(grow_in, grow, local.at[3, 3]),
    ]
    fixed = [
        pltpu.make_async_copy(fwd_in, fwd, local.at[2, 0]),
        pltpu.make_async_copy(inv_in, inv, local.at[2, 1]),
        pltpu.make_async_copy(turn_in.at[gy], turn, local.at[2, 2]),
        pltpu.make_async_copy(wind_in.at[gy], wind, local.at[2, 3]),
        pltpu.make_async_copy(table_in, table, local.at[3, 0]),
        pltpu.make_async_copy(cross_in, cross, local.at[3, 1]),
    ]
    start(own + small + fixed)
    barrier = pltpu.get_barrier_semaphore()
    for p in PEERS:
        pl.semaphore_signal(barrier, inc=1, device_id=device(p), device_id_type=MESH)

    pl.semaphore_wait(barrier, len(PEERS))
    b0_out = brick_copies(b_in, b0, xb, 3, halo_s.at[0], halo_r.at[0])
    r0_out = brick_copies(r_in, r0, xr, 2, halo_s.at[1], halo_r.at[1])
    b1_out = halo_copies(b1, (3, 4), (4, 8), (3, 4), halo_s.at[2], halo_r.at[2])
    r1_out = halo_copies(r1, (3, 4), (4, 8), (2, 2), halo_s.at[3], halo_r.at[3])
    xp0_out = halo_copies(xp0, (3, 4), (8, 16), (2, 2), halo_s.at[4], halo_r.at[4])
    xp1_out = halo_copies(xp1, (3, 4), (4, 8), (3, 3), halo_s.at[5], halo_r.at[5])
    start(b0_out)
    start(r0_out)

    def bricks(ref, k):
        for a, b in BRICKS:
            pltpu.make_async_remote_copy(
                ref.at[pl.ds(2 * gx, 2), pl.ds(4, 4), :],
                ref.at[pl.ds(2 * gx, 2), pl.ds(4 - 4 * b, 4), :],
                many_s.at[k],
                many_r.at[k],
                device_id=device((a, b)),
                device_id_type=MESH,
            ).start()

    def lines(ref, k):
        for _, b in LINE:
            pltpu.make_async_remote_copy(
                ref.at[pl.ds(32, 2), :],
                ref.at[pl.ds((32 - 2 * b) % 64, 2), :],
                many_s.at[k],
                many_r.at[k],
                device_id=device((0, b)),
                device_id_type=MESH,
            ).start()

    def all_of(ref, k):
        return pltpu.make_async_remote_copy(
            ref, ref, many_s.at[k], many_r.at[k], device_id=device((0, 1)), device_id_type=MESH
        )

    for c in small:
        c.wait()
    own[0].wait()

    @pl.loop(0, 8, unroll=True)
    def _(i):
        b0[i + 3, 4:20, :] = bs[i]

    def coarse0(planes, dst):
        tiles = [halve(thin, 4 * i, planes[i]) for i in range(4)]
        wide = [jnp.concatenate([tiles[i][t] for i in range(4)], axis=0) for t in range(4)]
        low = pick(jnp.concatenate(wide[:2], axis=1), pair[...])
        high = pick(jnp.concatenate(wide[2:], axis=1), pair[...])
        for i in range(4):
            dst[3 + i, 4:12, 0:128] = low[8 * i : 8 * i + 8]
            dst[3 + i, 4:12, 128:256] = high[8 * i : 8 * i + 8]
        return jnp.concatenate([low, high], axis=1)

    def coarse1(planes, dst):
        tiles = [halve(thin, 2 * i, planes[i]) for i in range(2)]
        wide = [jnp.concatenate([tiles[i][t] for i in range(2)], axis=0) for t in range(2)]
        low = pick(jnp.concatenate(wide, axis=1), pair[...])
        for i in range(2):
            dst[2 * gx + i, 4:8, :] = low[4 * i : 4 * i + 4]

    flat = coarse0([bs[2 * i] + bs[2 * i + 1] for i in range(4)], b1)
    coarse1([flat[16 * i : 16 * i + 8] + flat[16 * i + 8 : 16 * i + 16] for i in range(2)], b2)
    start(b1_out)
    bricks(b2, 0)
    own[1].wait()

    @pl.loop(0, 8, unroll=True)
    def _(i):
        r0[i + 3, 4:20, :] = rs[i]

    arrive(b0_out)
    arrive(r0_out)
    for i in range(3):
        b0[i, 4:20, :] = xb[i]
        b0[11 + i, 4:20, :] = xb[3 + i]
    for i in range(2):
        r0[1 + i, 4:20, :] = xr[i]
        r0[11 + i, 4:20, :] = xr[2 + i]

    row = iota((24, 512), 0)
    lane = iota((24, 512), 1)
    edge = jnp.where(gy == GY - 1, 19, jnp.where(gy == 0, 3, -1))
    mul_y = jnp.where(row == edge, 0.0, 2.0)
    mul_z = jnp.where(lane == 511, 0.0, 2.0)
    cut0 = jnp.where(gx == GX - 1, 10, jnp.where(gx == 0, 2, -1))

    wx0[0] = 2.0 * harm(b0[0], b0[1])

    @pl.loop(1, 13, unroll=UNROLL)
    def _(i):
        c = b0[i]
        wx = harm(c, b0[i + 1]) * jnp.where(i == cut0, 0.0, 2.0)
        wy = harm(c, up(c, 0)) * mul_y
        wz = harm(c, up(c, 1)) * mul_z
        wx0[i] = wx
        wy0[i] = wy
        wz0[i] = wz
        g = recip((wx + wx0[i - 1]) + (wy + down(wy, 0)) + (wz + down(wz, 1)))
        g0[i] = g
        d0[i] = g * r0[i] * C_FIRST

    def op0(ref, i):
        c = ref[i]
        fy = wy0[i] * (up(c, 0) - c)
        fz = wz0[i] * (up(c, 1) - c)
        fx = wx0[i] * (ref[i + 1] - c) - wx0[i - 1] * (c - ref[i - 1])
        return fx + (fy - down(fy, 0)) + (fz - down(fz, 1))

    @pl.loop(2, 12, unroll=UNROLL)
    def _(i):
        q = r0[i] + op0(d0, i)
        q0[i] = q
        e0[i] = C_OLD * d0[i] + C_NEW * (g0[i] * q)

    @pl.loop(3, 11, unroll=UNROLL)
    def _(i):
        q = q0[i] + op0(e0, i)
        q0[i] = q
        x = d0[i] + e0[i]
        xp0[i, 4:20, :] = x[4:20]

    coarse0([(q0[3 + 2 * i] + q0[4 + 2 * i])[4:20] for i in range(4)], r1)
    start(r1_out)
    start(xp0_out)

    arrive(b1_out)
    v = b1[...]
    shape = (10, 16, 256)
    edge = jnp.where(gy == GY - 1, 11, jnp.where(gy == 0, 3, -1))
    cut = jnp.where(gx == GX - 1, 6, jnp.where(gx == 0, 2, -1))
    keep_x = jnp.where(iota((9, 16, 256), 0) == cut, 0.0, 0.5)
    wx1 = harm(v[:-1], v[1:]) * keep_x
    wy1 = harm(v, up(v, 1)) * jnp.where(iota(shape, 1) == edge, 0.0, 0.5)
    wz1 = harm(v, up(v, 2)) * jnp.where(iota(shape, 2) == 255, 0.0, 0.5)
    c = slice(1, 9)
    g1 = recip(
        (wx1[1:] + wx1[:-1]) + (wy1[c] + down(wy1[c], 1)) + (wz1[c] + down(wz1[c], 2))
    )

    all_of(m2, 0).wait_recv()

    def to_flat(value):
        value = jnp.where(iota((16, 16, 128), 1) < 8, value, 0.0)
        wide = jnp.concatenate(
            [
                jnp.concatenate(
                    [value[4 * t] + value[4 * t + 1], value[4 * t + 2] + value[4 * t + 3]], axis=1
                )
                for t in range(4)
            ],
            axis=0,
        )
        wide = pick(wide, pair[...])
        tiles = [halve(thin, t, wide[16 * t : 16 * t + 16])[0][2:4] for t in range(4)]
        return jnp.concatenate(tiles, axis=1)

    v = b2[...]
    b3[32:34, :] = to_flat(v)
    lines(b3, 2)
    shape = (16, 16, 128)
    edge = jnp.where(gy == GY - 1, 7, jnp.where(gy == 0, 3, -1))
    scale = 2.0 * 4.0**-2
    wx2 = harm(v, jnp.concatenate([v[1:], v[:1]])) * jnp.where(iota(shape, 0) == 15, 0.0, scale)
    wy2 = harm(v, up(v, 1)) * jnp.where(iota(shape, 1) == edge, 0.0, scale)
    wz2 = harm(v, up(v, 2)) * jnp.where(iota(shape, 2) == 127, 0.0, scale)
    g2 = recip(
        (wx2 + jnp.concatenate([wx2[-1:], wx2[:-1]]))
        + (wy2 + down(wy2, 1))
        + (wz2 + down(wz2, 2))
    )

    arrive(r1_out)
    f1 = r1[...]
    d = g1 * f1[1:9] * C_FIRST
    q = f1[2:8] + planes_op(d, wx1[1:8], wy1[1:9], wz1[1:9], 1, 7)
    e = C_OLD * d[1:7] + C_NEW * (g1[1:7] * q)
    q = q[1:5] + planes_op(e, wx1[2:7], wy1[2:8], wz1[2:8], 1, 5)
    xp1[3:7, 4:12, :] = (d[2:6] + e[1:5])[:, 4:12, :]
    coarse1([(q[2 * i] + q[2 * i + 1])[4:12] for i in range(2)], r2)
    bricks(r2, 1)
    start(xp1_out)

    all_of(m3, 2).wait_recv()
    v = b3[...]
    shape = (64, 512)
    scale = 2.0 * 4.0**-3
    lane = iota(shape, 1)
    edge = lax.rem(95 - 2 * gy, 64)
    wx3 = harm(v, up(v, 1, 64)) * jnp.where(lane >= 448, 0.0, scale)
    wy3 = harm(v, up(v, 0)) * jnp.where(iota(shape, 0) == edge, 0.0, scale)
    wz3 = harm(v, up(v, 1)) * jnp.where(lax.rem(lane, 64) == 63, 0.0, scale)
    g3 = recip((wx3 + down(wx3, 1, 64)) + (wy3 + down(wy3, 0)) + (wz3 + down(wz3, 1)))

    all_of(m2, 1).wait_recv()
    f2 = r2[...]
    d = g2 * f2 * C_FIRST
    q = f2 + ring_op(d, wx2, wy2, wz2)
    e = C_OLD * d + C_NEW * (g2 * q)
    q = q + ring_op(e, wx2, wy2, wz2)
    xp2[:, 4:8, :] = (d + e)[:, 4:8, :]
    q = jnp.where(iota((16, 16, 128), 1) >= 4, q, 0.0)
    r3[32:34, :] = to_flat(q)
    lines(r3, 3)
    xp2_out = [
        pltpu.make_async_remote_copy(
            xp2.at[:, pl.ds(4, 4), :],
            xp2.at[:, pl.ds(4 - 4 * b, 4), :],
            halo_s.at[6, k],
            halo_r.at[6, k],
            device_id=device((0, b)),
            device_id_type=MESH,
        )
        for k, b in enumerate((-1, 1))
    ]
    start(xp2_out)

    for c in fixed:
        c.wait()
    all_of(m3, 3).wait_recv()
    f3 = r3[...]
    d = g3 * f3 * C_FIRST
    q = f3 + flat_op(d, wx3, wy3, wz3)
    e = C_OLD * d + C_NEW * (g3 * q)
    q = q + flat_op(e, wx3, wy3, wz3)
    t = jnp.concatenate([q[:, 128 * t : 128 * t + 128] for t in range(4)], axis=0)
    t = dot(t, fwd[...])
    t = jnp.concatenate([t[64 * i : 64 * i + 64] for i in range(4)], axis=1)
    t = jnp.concatenate(cross_x(t, cross, 0), axis=1)
    t = dot(turn[:, 0:64], t) * table[...]
    t = dot(wind[:, 0:64], t)
    t = dot(jnp.concatenate(cross_x(t, cross, 1), axis=0), inv[...])
    t = jnp.concatenate([t[16 * i : 16 * i + 16] for i in range(4)], axis=1)
    w = slice(24, 40)
    x = d[w] + e[w] + t
    w3 = (wx3[w], wy3[w], wz3[w])
    q = f3[w] + flat_op(x, *w3)
    d = g3[w] * q * C_FIRST
    q = q + flat_op(d, *w3)
    x = x + d + (C_OLD * d + C_NEW * (g3[w] * q))

    wide = pick(
        jnp.concatenate([x[:, 128 * t : 128 * t + 128] for t in range(4)], axis=0), grow[...]
    )
    wide = [double(thin, 2 * t, wide[16 * t : 16 * t + 16], 16, 16) for t in range(4)]
    wide = jnp.stack(
        [wide[i // 4][:, 128 * (i // 2 % 2) : 128 * (i // 2 % 2) + 128] for i in range(16)]
    )
    arrive(xp2_out)
    x = xp2[...] + wide
    q = f2 + ring_op(x, wx2, wy2, wz2)
    d = g2 * q * C_FIRST
    q = q + ring_op(d, wx2, wy2, wz2)
    x = x + d + (C_OLD * d + C_NEW * (g2 * q))
    e2[2:18] = x
    e2[0:2] = x[14:16]
    e2[18:20] = x[0:2]

    wide = pick(jnp.concatenate([e2[2 * gx + i] for i in range(6)], axis=0), grow[...])
    wide = [double(thin, 2 * i, wide[16 * i : 16 * i + 16], 8, 16) for i in range(6)]
    wide = jnp.stack([wide[(i + 1) // 2] for i in range(10)])
    arrive(xp1_out)
    x = xp1[...] + wide
    q = f1[1:9] + planes_op(x, wx1, wy1, wz1, 1, 9)
    d = g1 * q * C_FIRST
    q = q[1:7] + planes_op(d, wx1[1:8], wy1[1:9], wz1[1:9], 1, 7)
    x = x[2:8] + d[1:7] + (C_OLD * d[1:7] + C_NEW * (g1[1:7] * q))

    low = pick(jnp.concatenate([x[i, :, :128] for i in range(6)], axis=0), grow[...])
    high = pick(jnp.concatenate([x[i, :, 128:] for i in range(6)], axis=0), grow[...])
    wide = jnp.concatenate([low, high], axis=1)
    for i in range(6):
        y0[i] = double(thin, 4 * i, wide[16 * i : 16 * i + 16], 8, 24)
    arrive(xp0_out)

    @pl.loop(1, 13, unroll=UNROLL)
    def _(i):
        e0[i] = xp0[i] + y0[(i + 3) // 2 - 2]

    @pl.loop(2, 12, unroll=UNROLL)
    def _(i):
        q = r0[i] + op0(e0, i)
        q0[i] = q
        d0[i] = g0[i] * q * C_FIRST

    @pl.loop(3, 11, unroll=UNROLL)
    def _(i):
        q = q0[i] + op0(d0, i)
        d = d0[i]
        x = e0[i] + d + (C_OLD * d + C_NEW * (g0[i] * q))
        out[i - 3] = x[4:20]

    sent(b0_out + r0_out + b1_out + r1_out + xp0_out + xp1_out + xp2_out)
    all_of(m2, 0).wait_send()
    all_of(m2, 1).wait_send()
    all_of(m3, 2).wait_send()
    all_of(m3, 3).wait_send()


def local(right_side, inverse_density):
    consts = constants()
    far_spec = pl.BlockSpec(memory_space=pltpu.HBM)
    vmem_spec = pl.BlockSpec(memory_space=pltpu.VMEM)
    fine = pltpu.VMEM((14, 24, 512), F32)
    scratch = [pltpu.VMEM((8, 16, 512), F32)] * 2
    scratch += [pltpu.VMEM((6, 16, 512), F32), pltpu.VMEM((4, 16, 512), F32)]
    scratch += [fine] * 10 + [
        pltpu.VMEM((6, 24, 512), F32),
        pltpu.VMEM((24, 40, 128), F32),
        pltpu.VMEM((10, 16, 256), F32),
        pltpu.VMEM((10, 16, 256), F32),
        pltpu.VMEM((10, 16, 256), F32),
        pltpu.VMEM((16, 16, 128), F32),
        pltpu.VMEM((16, 16, 128), F32),
        pltpu.VMEM((16, 16, 128), F32),
        pltpu.VMEM((20, 16, 128), F32),
        pltpu.VMEM((len(BRICKS), 8, 128), F32),
        pltpu.VMEM((64, 512), F32),
        pltpu.VMEM((64, 512), F32),
        pltpu.VMEM((len(LINE), 8, 128), F32),
        pltpu.VMEM((128, 128), F32),
        pltpu.VMEM((128, 128), F32),
        pltpu.VMEM((64, 128), F32),
        pltpu.VMEM((16, 128), F32),
        pltpu.VMEM((64, 512), F32),
        pltpu.VMEM((64, 128), F32),
        pltpu.VMEM((256, 128), jnp.bfloat16),
        pltpu.VMEM((128, 256), jnp.bfloat16),
        pltpu.SemaphoreType.DMA((4, 4)),
        pltpu.SemaphoreType.DMA((7, 12)),
        pltpu.SemaphoreType.DMA((7, 12)),
        pltpu.SemaphoreType.DMA((4,)),
        pltpu.SemaphoreType.DMA((4,)),
    ]
    return pl.pallas_call(
        kernel,
        out_shape=jax.ShapeDtypeStruct((8, 16, 512), F32),
        in_specs=[far_spec] * 10,
        out_specs=vmem_spec,
        scratch_shapes=scratch,
        compiler_params=pltpu.CompilerParams(
            collective_id=0, has_side_effects=True, vmem_limit_bytes=63 * 2**20
        ),
    )(right_side, inverse_density, *consts)


def solution(mesh):
    return jax.shard_map(
        local,
        mesh=mesh,
        in_specs=(P("gx", "gy", None), P("gx", "gy", None)),
        out_specs=P("gx", "gy", None),
        check_vma=False,
    )
```

```python
import math
import numpy as np
import jax
import jax.numpy as jnp
from jax import lax
from jax.experimental import pallas as pl
from jax.experimental.pallas import tpu as pltpu
from jax.sharding import PartitionSpec as P

MESH = pl.DeviceIdType.MESH
F32 = jnp.float32
THETA = 1.25
DELTA = 0.75
SIGMA = THETA / DELTA
RHO0 = 1.0 / SIGMA
RHO1 = 1.0 / (2.0 * SIGMA - RHO0)
C_FIRST = 1.0 / THETA
C_OLD = RHO1 * RHO0
C_NEW = 2.0 * RHO1 / DELTA
GX, GY = 8, 32
UNROLL = True
NEIGHBOURS = [(a, b) for a in (-1, 0, 1) for b in (-1, 0, 1) if (a, b) != (0, 0)]
COLUMN = [(a, 0) for a in range(1, GX)]
LINE = [(0, b) for b in range(1, GY)]
ROUNDS = [
    [(1, 0), (-1, 0), (0, 1), (0, -1)],
    [(2, 0), (-2, 0), (0, 2), (0, -2)],
    [(0, 4), (0, -4)],
    [(0, 8), (0, -8)],
]


def dct_matrix(count):
    wave = np.arange(count)[:, None].astype(np.float64)
    place = np.arange(count)[None, :].astype(np.float64)
    norms = np.where(wave == 0, math.sqrt(1.0 / count), math.sqrt(2.0 / count))
    return norms * np.cos(np.pi * wave * (2 * place + 1) / (2 * count))


def constants():
    cy, cz = dct_matrix(64), dct_matrix(64)
    along = np.kron(np.eye(2), cz.T)
    turned = np.stack([np.roll(cy, 32 - 2 * g, axis=1) for g in range(GY)])
    window = np.stack([np.pad(t.T[24:40], ((0, 0), (0, 64))) for t in turned])
    turned = np.pad(turned, ((0, 0), (0, 0), (0, 64)))
    lam = [2 - 2 * np.cos(np.pi * np.arange(n) / n) for n in (8, 64, 64)]
    total = (lam[1][:, None, None] + lam[0][None, :, None] + lam[2][None, None, :]) * 4.0**-3
    total[0, 0, 0] = 1.0
    table = 1.0 / total
    table[0, 0, 0] = 0.0
    pair = np.zeros((256, 128))
    pair[np.arange(256), np.arange(256) // 2] = 0.125
    grow = np.zeros((128, 256))
    grow[np.arange(256) // 2, np.arange(256)] = 1.0
    cx = dct_matrix(8)
    cross = np.zeros((2, 2, 4, 4, 128))
    for i in range(4):
        for j in range(4):
            for k, c in enumerate((cx, cx.T)):
                cross[k, 0, i, j] = np.repeat([c[2 * i, 2 * j], c[2 * i + 1, 2 * j + 1]], 64)
                cross[k, 1, i, j] = np.repeat([c[2 * i, 2 * j + 1], c[2 * i + 1, 2 * j]], 64)
    out = (along, along.T, turned, window, table.reshape(64, 512), cross.reshape(64, 128))
    out = tuple(np.ascontiguousarray(v, dtype=np.float32) for v in out)
    return out + (pair.astype(jnp.bfloat16), grow.astype(jnp.bfloat16))


def device(offset):
    gx, gy = lax.axis_index("gx"), lax.axis_index("gy")
    return (lax.rem(gx + (offset[0] % GX), GX), lax.rem(gy + (offset[1] % GY), GY))


def recip(value):
    guess = pl.reciprocal(value, approx=True)
    return guess * (2.0 - value * guess)


def harm(a, b):
    return (a * b) * recip(a + b)


def up(value, axis, step=1):
    return pltpu.roll(value, value.shape[axis] - step, axis)


def down(value, axis, step=1):
    return pltpu.roll(value, step, axis)


def parts(value):
    high = value.astype(jnp.bfloat16)
    return high, (value - high.astype(F32)).astype(jnp.bfloat16)


def pick(value, matrix):
    high, low = parts(value)
    return jnp.dot(high, matrix, preferred_element_type=F32) + jnp.dot(
        low, matrix, preferred_element_type=F32
    )


def halve(ref, base, value):
    tiles = []
    for t in range(value.shape[-1] // 128):
        ref[base + t, 0 : value.shape[0], :] = value[:, 128 * t : 128 * t + 128]
        count = value.shape[0] // 2
        tiles.append(
            ref[base + t, pl.ds(0, count, stride=2), :] + ref[base + t, pl.ds(1, count, stride=2), :]
        )
    return tiles


def double(ref, base, value, at, low, count):
    n = value.shape[0]
    tiles = []
    for t in range(value.shape[-1] // 128):
        v = value[:, 128 * t : 128 * t + 128]
        ref[base + t, pl.ds(at, n, stride=2), :] = v
        ref[base + t, pl.ds(at + 1, n, stride=2), :] = v
        tiles.append(ref[base + t, low : low + count, :])
    return jnp.concatenate(tiles, axis=1)


def cross_x(value, cross, k):
    v = [value[:, 128 * t : 128 * t + 128] for t in range(4)]
    w = [pltpu.roll(t, 64, 1) for t in v]
    out = []
    for i in range(4):
        acc = None
        for j in range(4):
            row = 32 * k + 4 * i + j
            term = v[j] * cross[row : row + 1, :] + w[j] * cross[row + 16 : row + 17, :]
            acc = term if acc is None else acc + term
        out.append(acc)
    return out


def dot(a, b):
    return jnp.dot(a, b, precision=lax.Precision.HIGHEST, preferred_element_type=F32)


def iota(shape, axis):
    return lax.broadcasted_iota(jnp.int32, shape, axis)


def halo_copies(ref, at, size, halo, corner, send, recv):
    copies = []
    for a, b in NEIGHBOURS:
        take, put = [], []
        for side, s0, n, h in zip((a, b), at, size, corner if a != 0 and b != 0 else halo):
            if side == 0:
                take.append((s0, n))
                put.append(s0)
            elif side > 0:
                take.append((s0 + n - h, h))
                put.append(s0 - h)
            else:
                take.append((s0, h))
                put.append(s0 + n)
        (x_from, x_count), (y_from, y_count) = take
        y_end = y_from + y_count
        ends = [y_from] + list(range(y_from // 8 * 8 + 8, y_end, 8)) + [y_end]
        for low, high in zip(ends[:-1], ends[1:]):
            k = len(copies)
            copies.append(
                pltpu.make_async_remote_copy(
                    ref.at[pl.ds(x_from, x_count), pl.ds(low, high - low), :],
                    ref.at[pl.ds(put[0], x_count), pl.ds(put[1] + low - y_from, high - low), :],
                    send.at[k],
                    recv.at[k],
                    device_id=device((a, b)),
                    device_id_type=MESH,
                )
            )
    return copies


def brick_copies(src, dst, side, halo, send, recv):
    copies = []
    for k, (a, b) in enumerate(NEIGHBOURS):
        h = halo - 1 if a != 0 and b != 0 else halo
        x = {0: pl.ds(0, 8), 1: pl.ds(8 - h, h), -1: pl.ds(0, h)}[a]
        y = {0: pl.ds(0, 16), 1: pl.ds(16 - h, h), -1: pl.ds(0, h)}[b]
        if b == 0:
            to = side.at[pl.ds(0 if a > 0 else h, h), :, :]
        else:
            put_x = {0: pl.ds(3, 8), 1: pl.ds(3 - h, h), -1: pl.ds(11, h)}[a]
            put_y = {1: pl.ds(4 - h, h), -1: pl.ds(20, h)}[b]
            to = dst.at[put_x, put_y, :]
        copies.append(
            pltpu.make_async_remote_copy(
                src.at[x, y, :],
                to,
                send.at[k],
                recv.at[k],
                device_id=device((a, b)),
                device_id_type=MESH,
            )
        )
    return copies


def start(copies):
    for c in copies:
        c.start()


def arrive(copies):
    for c in copies:
        c.wait_recv()


def sent(copies):
    for c in copies:
        c.wait_send()


def planes_op(v, wx, wy, wz, lo, hi):
    c = v[lo:hi]
    fx = wx[lo - 1 : hi] * (v[lo : hi + 1] - v[lo - 1 : hi])
    fy = wy[lo:hi] * (up(c, 1) - c)
    fz = wz[lo:hi] * (up(c, 2) - c)
    return (fx[1:] - fx[:-1]) + (fy - down(fy, 1)) + (fz - down(fz, 2))


def ring_op(v, wx, wy, wz):
    fx = wx * (jnp.concatenate([v[1:], v[:1]]) - v)
    fy = wy * (up(v, 1) - v)
    fz = wz * (up(v, 2) - v)
    fx = fx - jnp.concatenate([fx[-1:], fx[:-1]])
    return fx + (fy - down(fy, 1)) + (fz - down(fz, 2))


def flat_op(v, wx, wy, wz):
    fx = wx * (up(v, 1, 64) - v)
    fy = wy * (up(v, 0) - v)
    fz = wz * (up(v, 1) - v)
    return (fx - down(fx, 1, 64)) + (fy - down(fy, 0)) + (fz - down(fz, 1))


def kernel(
    r_in, b_in, fwd_in, inv_in, turn_in, wind_in, table_in, cross_in, pair_in, grow_in, out,
    ov, bs, rs, xb, xr, b0, r0, wx0, wy0, wz0, g0, d0, e0, q0, xp0, y0, thin,
    b1, r1, xp1, b2, r2, xp2, rn2, e2, m2, b3, r3, m3,
    fwd, inv, turn, wind, table, cross, pair, grow,
    local, halo_s, halo_r, many_s, many_r, near, done,
):
    gx, gy = lax.axis_index("gx"), lax.axis_index("gy")
    own = [
        pltpu.make_async_copy(b_in, bs, local.at[0, 0]),
        pltpu.make_async_copy(r_in, rs, local.at[0, 1]),
    ]
    small = [
        pltpu.make_async_copy(pair_in, pair, local.at[3, 2]),
        pltpu.make_async_copy(grow_in, grow, local.at[3, 3]),
    ]
    fixed = [
        pltpu.make_async_copy(fwd_in, fwd, local.at[2, 0]),
        pltpu.make_async_copy(inv_in, inv, local.at[2, 1]),
        pltpu.make_async_copy(turn_in.at[gy], turn, local.at[2, 2]),
        pltpu.make_async_copy(wind_in.at[gy], wind, local.at[2, 3]),
        pltpu.make_async_copy(table_in, table, local.at[3, 0]),
        pltpu.make_async_copy(cross_in, cross, local.at[3, 1]),
    ]
    start(own + small + fixed)
    barrier = pltpu.get_barrier_semaphore()
    for p in NEIGHBOURS:
        pl.semaphore_signal(barrier, inc=1, device_id=device(p), device_id_type=MESH)

    pl.semaphore_wait(barrier, len(NEIGHBOURS))

    def tell(k):
        for p in ROUNDS[k]:
            pl.semaphore_signal(near.at[k], inc=1, device_id=device(p), device_id_type=MESH)

    def heard(k):
        pl.semaphore_wait(near.at[k], len(ROUNDS[k]))

    b0_out = brick_copies(b_in, b0, xb, 3, halo_s.at[0], halo_r.at[0])
    r0_out = brick_copies(r_in, r0, xr, 2, halo_s.at[1], halo_r.at[1])
    b1_out = halo_copies(b1, (3, 8), (4, 8), (3, 8), (3, 8), halo_s.at[2], halo_r.at[2])
    r1_out = halo_copies(r1, (3, 8), (4, 8), (2, 6), (2, 5), halo_s.at[3], halo_r.at[3])
    xp0_out = halo_copies(xp0, (3, 4), (8, 16), (2, 2), (1, 1), halo_s.at[4], halo_r.at[4])
    xp1_out = halo_copies(xp1, (3, 8), (4, 8), (3, 3), (3, 3), halo_s.at[5], halo_r.at[5])
    start(b0_out)
    start(r0_out)
    tell(0)

    def column(ref, k):
        for a, _ in COLUMN:
            pltpu.make_async_remote_copy(
                ref.at[pl.ds(2 * gx, 2)],
                ref.at[pl.ds(2 * gx, 2)],
                many_s.at[k],
                many_r.at[k],
                device_id=device((a, 0)),
                device_id_type=MESH,
            ).start()

    def lines(ref, k):
        for _, b in LINE:
            pltpu.make_async_remote_copy(
                ref.at[pl.ds(32, 2), :],
                ref.at[pl.ds((32 - 2 * b) % 64, 2), :],
                many_s.at[k],
                many_r.at[k],
                device_id=device((0, b)),
                device_id_type=MESH,
            ).start()

    def all_of(ref, k):
        return pltpu.make_async_remote_copy(
            ref, ref, many_s.at[k], many_r.at[k], device_id=device((0, 1)), device_id_type=MESH
        )

    for c in small:
        c.wait()
    own[0].wait()

    @pl.loop(0, 8, unroll=True)
    def _(i):
        b0[i + 3, 4:20, :] = bs[i]

    def coarse0(planes, dst):
        tiles = [halve(thin, 4 * i, planes[i]) for i in range(4)]
        wide = [jnp.concatenate([tiles[i][t] for i in range(4)], axis=0) for t in range(4)]
        low = pick(jnp.concatenate(wide[:2], axis=1), pair[...])
        high = pick(jnp.concatenate(wide[2:], axis=1), pair[...])
        for i in range(4):
            dst[3 + i, 8:16, 0:128] = low[8 * i : 8 * i + 8]
            dst[3 + i, 8:16, 128:256] = high[8 * i : 8 * i + 8]
        return jnp.concatenate([low, high], axis=1)

    def coarse1(planes, dst):
        tiles = [halve(thin, 2 * i, planes[i]) for i in range(2)]
        wide = [jnp.concatenate([tiles[i][t] for i in range(2)], axis=0) for t in range(2)]
        low = pick(jnp.concatenate(wide, axis=1), pair[...])
        for i in range(2):
            dst[2 * gx + i] = low[16 * i : 16 * i + 16]

    coarse0([bs[2 * i] + bs[2 * i + 1] for i in range(4)], b1)
    start(b1_out)
    own[1].wait()

    @pl.loop(0, 8, unroll=True)
    def _(i):
        r0[i + 3, 4:20, :] = rs[i]

    arrive(b0_out)
    arrive(r0_out)
    heard(0)
    tell(1)
    for i in range(3):
        b0[i, 4:20, :] = xb[i]
        b0[11 + i, 4:20, :] = xb[3 + i]
    for i in range(2):
        r0[1 + i, 4:20, :] = xr[i]
        r0[11 + i, 4:20, :] = xr[2 + i]

    row = iota((24, 512), 0)
    lane = iota((24, 512), 1)
    edge = jnp.where(gy == GY - 1, 19, jnp.where(gy == 0, 3, -1))
    mul_y = jnp.where(row == edge, 0.0, 2.0)
    mul_z = jnp.where(lane == 511, 0.0, 2.0)
    cut0 = jnp.where(gx == GX - 1, 10, jnp.where(gx == 0, 2, -1))

    wx0[0] = 2.0 * harm(b0[0], b0[1])

    @pl.loop(1, 13, unroll=UNROLL)
    def _(i):
        c = b0[i]
        wx = harm(c, b0[i + 1]) * jnp.where(i == cut0, 0.0, 2.0)
        wy = harm(c, up(c, 0)) * mul_y
        wz = harm(c, up(c, 1)) * mul_z
        wx0[i] = wx
        wy0[i] = wy
        wz0[i] = wz
        g = recip((wx + wx0[i - 1]) + (wy + down(wy, 0)) + (wz + down(wz, 1)))
        g0[i] = g
        d0[i] = g * r0[i] * C_FIRST

    def op0(ref, i):
        c = ref[i]
        fy = wy0[i] * (up(c, 0) - c)
        fz = wz0[i] * (up(c, 1) - c)
        fx = wx0[i] * (ref[i + 1] - c) - wx0[i - 1] * (c - ref[i - 1])
        return fx + (fy - down(fy, 0)) + (fz - down(fz, 1))

    @pl.loop(2, 12, unroll=UNROLL)
    def _(i):
        q = r0[i] + op0(d0, i)
        q0[i] = q
        e0[i] = C_OLD * d0[i] + C_NEW * (g0[i] * q)

    @pl.loop(3, 11, unroll=UNROLL)
    def _(i):
        q = q0[i] + op0(e0, i)
        q0[i] = q
        x = d0[i] + e0[i]
        xp0[i, 4:20, :] = x[4:20]

    coarse0([(q0[3 + 2 * i] + q0[4 + 2 * i])[4:20] for i in range(4)], r1)
    start(r1_out)
    heard(1)
    tell(2)

    arrive(b1_out)
    v = b1[...]
    blank = jnp.zeros((8, 256), F32)

    def tall(value):
        return jnp.concatenate([value, blank], axis=0)

    coarse1([tall(v[3 + 2 * i] + v[4 + 2 * i]) for i in range(2)], b2)
    column(b2, 0)
    shape = (10, 24, 256)
    edge = jnp.where(gy == GY - 1, 15, jnp.where(gy == 0, 7, -1))
    cut = jnp.where(gx == GX - 1, 6, jnp.where(gx == 0, 2, -1))
    keep_x = jnp.where(iota((9, 24, 256), 0) == cut, 0.0, 0.5)
    wx1 = harm(v[:-1], v[1:]) * keep_x
    wy1 = harm(v, up(v, 1)) * jnp.where(iota(shape, 1) == edge, 0.0, 0.5)
    wz1 = harm(v, up(v, 2)) * jnp.where(iota(shape, 2) == 255, 0.0, 0.5)
    c = slice(1, 9)
    g1 = recip(
        (wx1[1:] + wx1[:-1]) + (wy1[c] + down(wy1[c], 1)) + (wz1[c] + down(wz1[c], 2))
    )

    arrive(r1_out)
    heard(2)
    tell(3)
    f1 = r1[...]
    d = g1 * f1[1:9] * C_FIRST
    q = f1[2:8] + planes_op(d, wx1[1:8], wy1[1:9], wz1[1:9], 1, 7)
    e = C_OLD * d[1:7] + C_NEW * (g1[1:7] * q)
    q = q[1:5] + planes_op(e, wx1[2:7], wy1[2:8], wz1[2:8], 1, 5)
    xp1[3:7, 8:16, :] = (d[2:6] + e[1:5])[:, 8:16, :]
    line = iota((24, 256), 0)
    inside = (line >= 4) & (line < 20)
    coarse1([tall(jnp.where(inside, q[2 * i] + q[2 * i + 1], 0.0)) for i in range(2)], r2)
    column(r2, 1)

    all_of(m2, 0).wait_recv()

    def to_flat(value):
        value = jnp.where(iota((16, 16, 128), 1) < 8, value, 0.0)
        wide = jnp.concatenate(
            [
                jnp.concatenate(
                    [value[4 * t] + value[4 * t + 1], value[4 * t + 2] + value[4 * t + 3]], axis=1
                )
                for t in range(4)
            ],
            axis=0,
        )
        wide = pick(wide, pair[...])
        tiles = [halve(thin, t, wide[16 * t : 16 * t + 16])[0][2:4] for t in range(4)]
        return jnp.concatenate(tiles, axis=1)

    v = b2[...]
    b3[32:34, :] = to_flat(v)
    heard(3)
    lines(b3, 2)
    shape = (16, 16, 128)
    edge = jnp.where(gy == GY - 1, 7, jnp.where(gy == 0, 3, -1))
    scale = 2.0 * 4.0**-2
    wx2 = harm(v, jnp.concatenate([v[1:], v[:1]])) * jnp.where(iota(shape, 0) == 15, 0.0, scale)
    wy2 = harm(v, up(v, 1)) * jnp.where(iota(shape, 1) == edge, 0.0, scale)
    wz2 = harm(v, up(v, 2)) * jnp.where(iota(shape, 2) == 127, 0.0, scale)
    g2 = recip(
        (wx2 + jnp.concatenate([wx2[-1:], wx2[:-1]]))
        + (wy2 + down(wy2, 1))
        + (wz2 + down(wz2, 2))
    )

    all_of(m2, 1).wait_recv()
    f2 = r2[...]
    d = g2 * f2 * C_FIRST
    q = f2 + ring_op(d, wx2, wy2, wz2)
    e = C_OLD * d + C_NEW * (g2 * q)
    q = q + ring_op(e, wx2, wy2, wz2)
    xp2[:, 4:8, :] = (d + e)[:, 4:8, :]
    rn2[:, 4:8, :] = f2[:, 4:8, :]
    q = jnp.where(iota((16, 16, 128), 1) >= 4, q, 0.0)
    r3[32:34, :] = to_flat(q)
    lines(r3, 3)
    xp2_out = [
        pltpu.make_async_remote_copy(
            ref.at[:, pl.ds(4, 4), :],
            ref.at[:, pl.ds(4 - 4 * b, 4), :],
            halo_s.at[6, 2 * j + k],
            halo_r.at[6, 2 * j + k],
            device_id=device((0, b)),
            device_id_type=MESH,
        )
        for j, ref in enumerate((xp2, rn2))
        for k, b in enumerate((-1, 1))
    ]
    start(xp2_out)
    start(xp1_out)
    start(xp0_out)

    all_of(m3, 2).wait_recv()
    v = b3[...]
    shape = (64, 512)
    scale = 2.0 * 4.0**-3
    lane = iota(shape, 1)
    edge = lax.rem(95 - 2 * gy, 64)
    wx3 = harm(v, up(v, 1, 64)) * jnp.where(lane >= 448, 0.0, scale)
    wy3 = harm(v, up(v, 0)) * jnp.where(iota(shape, 0) == edge, 0.0, scale)
    wz3 = harm(v, up(v, 1)) * jnp.where(lax.rem(lane, 64) == 63, 0.0, scale)
    g3 = recip((wx3 + down(wx3, 1, 64)) + (wy3 + down(wy3, 0)) + (wz3 + down(wz3, 1)))

    sent(b0_out + r0_out + b1_out + r1_out)
    all_of(m2, 0).wait_send()
    all_of(m2, 1).wait_send()
    all_of(m3, 2).wait_send()

    for c in fixed:
        c.wait()
    all_of(m3, 3).wait_recv()
    f3 = r3[...]
    d = g3 * f3 * C_FIRST
    q = f3 + flat_op(d, wx3, wy3, wz3)
    e = C_OLD * d + C_NEW * (g3 * q)
    q = q + flat_op(e, wx3, wy3, wz3)
    t = jnp.concatenate([q[:, 128 * t : 128 * t + 128] for t in range(4)], axis=0)
    t = dot(t, fwd[...])
    t = jnp.concatenate([t[64 * i : 64 * i + 64] for i in range(4)], axis=1)
    t = jnp.concatenate(cross_x(t, cross, 0), axis=1)
    t = dot(turn[:, 0:64], t) * table[...]
    t = dot(wind[:, 0:64], t)
    t = dot(jnp.concatenate(cross_x(t, cross, 1), axis=0), inv[...])
    t = jnp.concatenate([t[16 * i : 16 * i + 16] for i in range(4)], axis=1)
    w = slice(24, 40)
    x = d[w] + e[w] + t
    w3 = (wx3[w], wy3[w], wz3[w])
    q = f3[w] + flat_op(x, *w3)
    d = g3[w] * q * C_FIRST
    q = q + flat_op(d, *w3)
    x = x + d + (C_OLD * d + C_NEW * (g3[w] * q))

    wide = pick(
        jnp.concatenate([x[:, 128 * t : 128 * t + 128] for t in range(4)], axis=0), grow[...]
    )
    wide = [double(thin, 2 * t, wide[16 * t : 16 * t + 16], 4, 16, 16) for t in range(4)]
    wide = jnp.stack(
        [wide[i // 4][:, 128 * (i // 2 % 2) : 128 * (i // 2 % 2) + 128] for i in range(16)]
    )
    arrive(xp2_out)
    x = xp2[...] + wide
    q = rn2[...] + ring_op(x, wx2, wy2, wz2)
    d = g2 * q * C_FIRST
    q = q + ring_op(d, wx2, wy2, wz2)
    x = x + d + (C_OLD * d + C_NEW * (g2 * q))
    e2[2:18] = x
    e2[0:2] = x[14:16]
    e2[18:20] = x[0:2]

    wide = pick(jnp.concatenate([e2[2 * gx + i] for i in range(6)], axis=0), grow[...])
    wide = [double(thin, 2 * i, wide[16 * i : 16 * i + 16], 0, 0, 24) for i in range(6)]
    wide = jnp.stack([wide[(i + 1) // 2] for i in range(10)])
    arrive(xp1_out)
    x = xp1[...] + wide
    q = f1[1:9] + planes_op(x, wx1, wy1, wz1, 1, 9)
    d = g1 * q * C_FIRST
    q = q[1:7] + planes_op(d, wx1[1:8], wy1[1:9], wz1[1:9], 1, 7)
    x = x[2:8] + d[1:7] + (C_OLD * d[1:7] + C_NEW * (g1[1:7] * q))

    low = pick(jnp.concatenate([x[i, :, :128] for i in range(6)], axis=0), grow[...])
    high = pick(jnp.concatenate([x[i, :, 128:] for i in range(6)], axis=0), grow[...])
    wide = jnp.concatenate([low, high], axis=1)
    for i in range(6):
        y0[i] = double(thin, 4 * i, wide[24 * i : 24 * i + 24], 4, 16, 24)
    arrive(xp0_out)
    sent(xp0_out + xp1_out + xp2_out)
    all_of(m3, 3).wait_send()

    @pl.loop(1, 13, unroll=UNROLL)
    def _(i):
        e0[i] = xp0[i] + y0[(i + 3) // 2 - 2]

    @pl.loop(2, 12, unroll=UNROLL)
    def _(i):
        q = r0[i] + op0(e0, i)
        q0[i] = q
        d0[i] = g0[i] * q * C_FIRST

    @pl.loop(3, 11, unroll=UNROLL)
    def _(i):
        q = q0[i] + op0(d0, i)
        d = d0[i]
        x = e0[i] + d + (C_OLD * d + C_NEW * (g0[i] * q))
        ov[i - 3] = x[4:20]
        pltpu.make_async_copy(ov.at[i - 3], out.at[i - 3], done.at[i - 3]).start()

    for i in range(8):
        pltpu.make_async_copy(ov.at[i], out.at[i], done.at[i]).wait()


def local(right_side, inverse_density):
    consts = constants()
    far_spec = pl.BlockSpec(memory_space=pltpu.HBM)
    fine = pltpu.VMEM((14, 24, 512), F32)
    scratch = [pltpu.VMEM((8, 16, 512), F32)] * 3
    scratch += [pltpu.VMEM((6, 16, 512), F32), pltpu.VMEM((4, 16, 512), F32)]
    scratch += [fine] * 10 + [
        pltpu.VMEM((6, 24, 512), F32),
        pltpu.VMEM((24, 56, 128), F32),
        pltpu.VMEM((10, 24, 256), F32),
        pltpu.VMEM((10, 24, 256), F32),
        pltpu.VMEM((10, 24, 256), F32),
        pltpu.VMEM((16, 16, 128), F32),
        pltpu.VMEM((16, 16, 128), F32),
        pltpu.VMEM((16, 16, 128), F32),
        pltpu.VMEM((16, 16, 128), F32),
        pltpu.VMEM((20, 16, 128), F32),
        pltpu.VMEM((2 * len(COLUMN), 16, 128), F32),
        pltpu.VMEM((64, 512), F32),
        pltpu.VMEM((64, 512), F32),
        pltpu.VMEM((len(LINE), 8, 128), F32),
        pltpu.VMEM((128, 128), F32),
        pltpu.VMEM((128, 128), F32),
        pltpu.VMEM((64, 128), F32),
        pltpu.VMEM((16, 128), F32),
        pltpu.VMEM((64, 512), F32),
        pltpu.VMEM((64, 128), F32),
        pltpu.VMEM((256, 128), jnp.bfloat16),
        pltpu.VMEM((128, 256), jnp.bfloat16),
        pltpu.SemaphoreType.DMA((4, 4)),
        pltpu.SemaphoreType.DMA((7, 12)),
        pltpu.SemaphoreType.DMA((7, 12)),
        pltpu.SemaphoreType.DMA((4,)),
        pltpu.SemaphoreType.DMA((4,)),
        pltpu.SemaphoreType.REGULAR((4,)),
        pltpu.SemaphoreType.DMA((8,)),
    ]
    return pl.pallas_call(
        kernel,
        out_shape=jax.ShapeDtypeStruct((8, 16, 512), F32),
        in_specs=[far_spec] * 10,
        out_specs=far_spec,
        scratch_shapes=scratch,
        compiler_params=pltpu.CompilerParams(
            collective_id=0, has_side_effects=True, vmem_limit_bytes=63 * 2**20
        ),
    )(right_side, inverse_density, *consts)


def solution(mesh):
    return jax.shard_map(
        local,
        mesh=mesh,
        in_specs=(P("gx", "gy", None), P("gx", "gy", None)),
        out_specs=P("gx", "gy", None),
        check_vma=False,
    )
```

```python
import math
import numpy as np
import jax
import jax.numpy as jnp
from jax import lax
from jax.experimental import pallas as pl
from jax.experimental.pallas import tpu as pltpu
from jax.sharding import PartitionSpec as P

MESH = pl.DeviceIdType.MESH
F32 = jnp.float32
THETA = 1.25
DELTA = 0.75
SIGMA = THETA / DELTA
RHO0 = 1.0 / SIGMA
RHO1 = 1.0 / (2.0 * SIGMA - RHO0)
C_FIRST = 1.0 / THETA
C_OLD = RHO1 * RHO0
C_NEW = 2.0 * RHO1 / DELTA
GX, GY = 8, 32
UNROLL = True
NEIGHBOURS = [(1, 1), (1, -1), (-1, 1), (-1, -1), (0, 1), (0, -1), (1, 0), (-1, 0)]
COLUMN = [(a, 0) for a in (4, 5, 3, 6, 2, 7, 1)]


def hops(b):
    z = b % 8
    x = b // 8
    near = min(z, 8 - z) + min(x, 4 - x)
    x = (x + 1) % 4
    return near + min(z, 8 - z) + min(x, 4 - x) if z else 2 * near


LINE = sorted([(0, b) for b in range(1, GY)], key=lambda p: -hops(p[1]))
ROUNDS = [
    [(1, 0), (-1, 0), (0, 1), (0, -1)],
    [(2, 0), (-2, 0), (0, 2), (0, -2)],
    [(0, 4), (0, -4)],
    [(0, 8), (0, -8)],
]


def dct_matrix(count):
    wave = np.arange(count)[:, None].astype(np.float64)
    place = np.arange(count)[None, :].astype(np.float64)
    norms = np.where(wave == 0, math.sqrt(1.0 / count), math.sqrt(2.0 / count))
    return norms * np.cos(np.pi * wave * (2 * place + 1) / (2 * count))


def constants():
    cy, cz = dct_matrix(64), dct_matrix(64)
    along = np.kron(np.eye(2), cz.T)
    turned = np.stack([np.roll(cy, 32 - 2 * g, axis=1) for g in range(GY)])
    window = np.stack([np.pad(t.T[24:40], ((0, 0), (0, 64))) for t in turned])
    turned = np.pad(turned, ((0, 0), (0, 0), (0, 64)))
    lam = [2 - 2 * np.cos(np.pi * np.arange(n) / n) for n in (8, 64, 64)]
    total = (lam[1][:, None, None] + lam[0][None, :, None] + lam[2][None, None, :]) * 4.0**-3
    total[0, 0, 0] = 1.0
    table = 1.0 / total
    table[0, 0, 0] = 0.0
    pair = np.zeros((256, 128))
    pair[np.arange(256), np.arange(256) // 2] = 0.125
    grow = np.zeros((128, 256))
    grow[np.arange(256) // 2, np.arange(256)] = 1.0
    cx = dct_matrix(8)
    cross = np.zeros((2, 2, 4, 4, 128))
    for i in range(4):
        for j in range(4):
            for k, c in enumerate((cx, cx.T)):
                cross[k, 0, i, j] = np.repeat([c[2 * i, 2 * j], c[2 * i + 1, 2 * j + 1]], 64)
                cross[k, 1, i, j] = np.repeat([c[2 * i, 2 * j + 1], c[2 * i + 1, 2 * j]], 64)
    out = (along, along.T, turned, window, table.reshape(64, 512), cross.reshape(64, 128))
    out = tuple(np.ascontiguousarray(v, dtype=np.float32) for v in out)
    return out + (pair.astype(jnp.bfloat16), grow.astype(jnp.bfloat16))


def device(offset):
    gx, gy = lax.axis_index("gx"), lax.axis_index("gy")
    return (lax.rem(gx + (offset[0] % GX), GX), lax.rem(gy + (offset[1] % GY), GY))


def recip(value):
    guess = pl.reciprocal(value, approx=True)
    return guess * (2.0 - value * guess)


def harm(a, b):
    return (a * b) * recip(a + b)


def up(value, axis, step=1):
    return pltpu.roll(value, value.shape[axis] - step, axis)


def down(value, axis, step=1):
    return pltpu.roll(value, step, axis)


def parts(value):
    high = value.astype(jnp.bfloat16)
    return high, (value - high.astype(F32)).astype(jnp.bfloat16)


def pick(value, matrix):
    high, low = parts(value)
    return jnp.dot(high, matrix, preferred_element_type=F32) + jnp.dot(
        low, matrix, preferred_element_type=F32
    )


def halve(ref, base, value):
    tiles = []
    for t in range(value.shape[-1] // 128):
        ref[base + t, 0 : value.shape[0], :] = value[:, 128 * t : 128 * t + 128]
        count = value.shape[0] // 2
        tiles.append(
            ref[base + t, pl.ds(0, count, stride=2), :] + ref[base + t, pl.ds(1, count, stride=2), :]
        )
    return tiles


def double(ref, base, value, at, low, count):
    n = value.shape[0]
    tiles = []
    for t in range(value.shape[-1] // 128):
        v = value[:, 128 * t : 128 * t + 128]
        ref[base + t, pl.ds(at, n, stride=2), :] = v
        ref[base + t, pl.ds(at + 1, n, stride=2), :] = v
        tiles.append(ref[base + t, low : low + count, :])
    return jnp.concatenate(tiles, axis=1)


def cross_x(value, cross, k):
    v = [value[:, 128 * t : 128 * t + 128] for t in range(4)]
    w = [pltpu.roll(t, 64, 1) for t in v]
    out = []
    for i in range(4):
        acc = None
        for j in range(4):
            row = 32 * k + 4 * i + j
            term = v[j] * cross[row : row + 1, :] + w[j] * cross[row + 16 : row + 17, :]
            acc = term if acc is None else acc + term
        out.append(acc)
    return out


def dot(a, b):
    return jnp.dot(a, b, precision=lax.Precision.HIGHEST, preferred_element_type=F32)


def iota(shape, axis):
    return lax.broadcasted_iota(jnp.int32, shape, axis)


def halo_copies(ref, at, size, halo, corner, send, recv):
    copies = []
    for a, b in NEIGHBOURS:
        take, put = [], []
        for side, s0, n, h in zip((a, b), at, size, corner if a != 0 and b != 0 else halo):
            if side == 0:
                take.append((s0, n))
                put.append(s0)
            elif side > 0:
                take.append((s0 + n - h, h))
                put.append(s0 - h)
            else:
                take.append((s0, h))
                put.append(s0 + n)
        (x_from, x_count), (y_from, y_count) = take
        y_end = y_from + y_count
        ends = [y_from] + list(range(y_from // 8 * 8 + 8, y_end, 8)) + [y_end]
        for low, high in zip(ends[:-1], ends[1:]):
            k = len(copies)
            copies.append(
                pltpu.make_async_remote_copy(
                    ref.at[pl.ds(x_from, x_count), pl.ds(low, high - low), :],
                    ref.at[pl.ds(put[0], x_count), pl.ds(put[1] + low - y_from, high - low), :],
                    send.at[k],
                    recv.at[k],
                    device_id=device((a, b)),
                    device_id_type=MESH,
                )
            )
    return copies


def brick_copies(src, dst, side, halo, send, recv):
    copies = []
    for k, (a, b) in enumerate(NEIGHBOURS):
        h = halo - 1 if a != 0 and b != 0 else halo
        x = {0: pl.ds(0, 8), 1: pl.ds(8 - h, h), -1: pl.ds(0, h)}[a]
        y = {0: pl.ds(0, 16), 1: pl.ds(16 - h, h), -1: pl.ds(0, h)}[b]
        if b == 0:
            to = side.at[pl.ds(0 if a > 0 else h, h), :, :]
        else:
            put_x = {0: pl.ds(3, 8), 1: pl.ds(3 - h, h), -1: pl.ds(11, h)}[a]
            put_y = {1: pl.ds(4 - h, h), -1: pl.ds(20, h)}[b]
            to = dst.at[put_x, put_y, :]
        copies.append(
            pltpu.make_async_remote_copy(
                src.at[x, y, :],
                to,
                send.at[k],
                recv.at[k],
                device_id=device((a, b)),
                device_id_type=MESH,
            )
        )
    return copies


def start(copies):
    for c in copies:
        c.start()


def arrive(copies):
    for c in copies:
        c.wait_recv()


def sent(copies):
    for c in copies:
        c.wait_send()


def planes_op(v, wx, wy, wz, lo, hi):
    c = v[lo:hi]
    fx = wx[lo - 1 : hi] * (v[lo : hi + 1] - v[lo - 1 : hi])
    fy = wy[lo:hi] * (up(c, 1) - c)
    fz = wz[lo:hi] * (up(c, 2) - c)
    return (fx[1:] - fx[:-1]) + (fy - down(fy, 1)) + (fz - down(fz, 2))


def ring_op(v, wx, wy, wz):
    fx = wx * (jnp.concatenate([v[1:], v[:1]]) - v)
    fy = wy * (up(v, 1) - v)
    fz = wz * (up(v, 2) - v)
    fx = fx - jnp.concatenate([fx[-1:], fx[:-1]])
    return fx + (fy - down(fy, 1)) + (fz - down(fz, 2))


def flat_op(v, wx, wy, wz):
    fx = wx * (up(v, 1, 64) - v)
    fy = wy * (up(v, 0) - v)
    fz = wz * (up(v, 1) - v)
    return (fx - down(fx, 1, 64)) + (fy - down(fy, 0)) + (fz - down(fz, 1))


def kernel(
    r_in, b_in, fwd_in, inv_in, turn_in, wind_in, table_in, cross_in, pair_in, grow_in, out,
    ov, bs, rs, xb, xr, b0, r0, wx0, wy0, wz0, g0, d0, e0, q0, xp0, y0, thin,
    b1, r1, xp1, b2, r2, xp2, rn2, e2, m2, b3, r3, m3,
    fwd, inv, turn, wind, table, cross, pair, grow,
    local, halo_s, halo_r, many_s, many_r, near, done,
):
    gx, gy = lax.axis_index("gx"), lax.axis_index("gy")
    own = [
        pltpu.make_async_copy(b_in, bs, local.at[0, 0]),
        pltpu.make_async_copy(r_in, rs, local.at[0, 1]),
    ]
    small = [
        pltpu.make_async_copy(pair_in, pair, local.at[3, 2]),
        pltpu.make_async_copy(grow_in, grow, local.at[3, 3]),
    ]
    fixed = [
        pltpu.make_async_copy(fwd_in, fwd, local.at[2, 0]),
        pltpu.make_async_copy(inv_in, inv, local.at[2, 1]),
        pltpu.make_async_copy(turn_in.at[gy], turn, local.at[2, 2]),
        pltpu.make_async_copy(wind_in.at[gy], wind, local.at[2, 3]),
        pltpu.make_async_copy(table_in, table, local.at[3, 0]),
        pltpu.make_async_copy(cross_in, cross, local.at[3, 1]),
    ]
    barrier = pltpu.get_barrier_semaphore()
    for p in NEIGHBOURS:
        pl.semaphore_signal(barrier, inc=1, device_id=device(p), device_id_type=MESH)

    pl.semaphore_wait(barrier, len(NEIGHBOURS))

    def tell(k):
        for p in ROUNDS[k]:
            pl.semaphore_signal(near.at[k], inc=1, device_id=device(p), device_id_type=MESH)

    def heard(k):
        pl.semaphore_wait(near.at[k], len(ROUNDS[k]))

    b0_out = brick_copies(b_in, b0, xb, 3, halo_s.at[0], halo_r.at[0])
    r0_out = brick_copies(r_in, r0, xr, 2, halo_s.at[1], halo_r.at[1])
    b1_out = halo_copies(b1, (3, 8), (4, 8), (3, 8), (3, 8), halo_s.at[2], halo_r.at[2])
    r1_out = halo_copies(r1, (3, 8), (4, 8), (2, 6), (2, 5), halo_s.at[3], halo_r.at[3])
    xp0_out = halo_copies(xp0, (3, 4), (8, 16), (2, 2), (1, 1), halo_s.at[4], halo_r.at[4])
    xp1_out = halo_copies(xp1, (3, 8), (4, 8), (3, 3), (3, 3), halo_s.at[5], halo_r.at[5])
    start(b0_out[:4] + r0_out[:4] + b0_out[4:6] + r0_out[4:6] + b0_out[6:] + r0_out[6:])
    tell(0)
    start(own + small + fixed)

    def column(ref, k):
        for a, _ in COLUMN:
            pltpu.make_async_remote_copy(
                ref.at[pl.ds(2 * gx, 2)],
                ref.at[pl.ds(2 * gx, 2)],
                many_s.at[k],
                many_r.at[k],
                device_id=device((a, 0)),
                device_id_type=MESH,
            ).start()

    def lines(ref, k):
        for _, b in LINE:
            pltpu.make_async_remote_copy(
                ref.at[pl.ds(32, 2), :],
                ref.at[pl.ds((32 - 2 * b) % 64, 2), :],
                many_s.at[k],
                many_r.at[k],
                device_id=device((0, b)),
                device_id_type=MESH,
            ).start()

    def all_of(ref, k):
        return pltpu.make_async_remote_copy(
            ref, ref, many_s.at[k], many_r.at[k], device_id=device((0, 1)), device_id_type=MESH
        )

    for c in small:
        c.wait()
    own[0].wait()

    @pl.loop(0, 8, unroll=True)
    def _(i):
        b0[i + 3, 4:20, :] = bs[i]

    def coarse0(planes, dst):
        tiles = [halve(thin, 4 * i, planes[i]) for i in range(4)]
        wide = [jnp.concatenate([tiles[i][t] for i in range(4)], axis=0) for t in range(4)]
        low = pick(jnp.concatenate(wide[:2], axis=1), pair[...])
        high = pick(jnp.concatenate(wide[2:], axis=1), pair[...])
        for i in range(4):
            dst[3 + i, 8:16, 0:128] = low[8 * i : 8 * i + 8]
            dst[3 + i, 8:16, 128:256] = high[8 * i : 8 * i + 8]
        return jnp.concatenate([low, high], axis=1)

    def coarse1(planes, dst):
        tiles = [halve(thin, 2 * i, planes[i]) for i in range(2)]
        wide = [jnp.concatenate([tiles[i][t] for i in range(2)], axis=0) for t in range(2)]
        low = pick(jnp.concatenate(wide, axis=1), pair[...])
        for i in range(2):
            dst[2 * gx + i] = low[16 * i : 16 * i + 16]

    coarse0([bs[2 * i] + bs[2 * i + 1] for i in range(4)], b1)
    start(b1_out)
    own[1].wait()

    @pl.loop(0, 8, unroll=True)
    def _(i):
        r0[i + 3, 4:20, :] = rs[i]

    arrive(b0_out)
    arrive(r0_out)
    heard(0)
    tell(1)
    for i in range(3):
        b0[i, 4:20, :] = xb[i]
        b0[11 + i, 4:20, :] = xb[3 + i]
    for i in range(2):
        r0[1 + i, 4:20, :] = xr[i]
        r0[11 + i, 4:20, :] = xr[2 + i]

    row = iota((24, 512), 0)
    lane = iota((24, 512), 1)
    edge = jnp.where(gy == GY - 1, 19, jnp.where(gy == 0, 3, -1))
    mul_y = jnp.where(row == edge, 0.0, 2.0)
    mul_z = jnp.where(lane == 511, 0.0, 2.0)
    cut0 = jnp.where(gx == GX - 1, 10, jnp.where(gx == 0, 2, -1))

    wx0[0] = 2.0 * harm(b0[0], b0[1])

    @pl.loop(1, 13, unroll=UNROLL)
    def _(i):
        c = b0[i]
        wx = harm(c, b0[i + 1]) * jnp.where(i == cut0, 0.0, 2.0)
        wy = harm(c, up(c, 0)) * mul_y
        wz = harm(c, up(c, 1)) * mul_z
        wx0[i] = wx
        wy0[i] = wy
        wz0[i] = wz
        g = recip((wx + wx0[i - 1]) + (wy + down(wy, 0)) + (wz + down(wz, 1)))
        g0[i] = g
        d0[i] = g * r0[i] * C_FIRST

    def op0(ref, i):
        c = ref[i]
        fy = wy0[i] * (up(c, 0) - c)
        fz = wz0[i] * (up(c, 1) - c)
        fx = wx0[i] * (ref[i + 1] - c) - wx0[i - 1] * (c - ref[i - 1])
        return fx + (fy - down(fy, 0)) + (fz - down(fz, 1))

    @pl.loop(2, 12, unroll=UNROLL)
    def _(i):
        q = r0[i] + op0(d0, i)
        q0[i] = q
        e0[i] = C_OLD * d0[i] + C_NEW * (g0[i] * q)

    @pl.loop(3, 11, unroll=UNROLL)
    def _(i):
        q = q0[i] + op0(e0, i)
        q0[i] = q
        x = d0[i] + e0[i]
        xp0[i, 4:20, :] = x[4:20]

    coarse0([(q0[3 + 2 * i] + q0[4 + 2 * i])[4:20] for i in range(4)], r1)
    start(r1_out)
    heard(1)
    tell(2)

    arrive(b1_out)
    v = b1[...]
    blank = jnp.zeros((8, 256), F32)

    def tall(value):
        return jnp.concatenate([value, blank], axis=0)

    coarse1([tall(v[3 + 2 * i] + v[4 + 2 * i]) for i in range(2)], b2)
    column(b2, 0)
    shape = (10, 24, 256)
    edge = jnp.where(gy == GY - 1, 15, jnp.where(gy == 0, 7, -1))
    cut = jnp.where(gx == GX - 1, 6, jnp.where(gx == 0, 2, -1))
    keep_x = jnp.where(iota((9, 24, 256), 0) == cut, 0.0, 0.5)
    wx1 = harm(v[:-1], v[1:]) * keep_x
    wy1 = harm(v, up(v, 1)) * jnp.where(iota(shape, 1) == edge, 0.0, 0.5)
    wz1 = harm(v, up(v, 2)) * jnp.where(iota(shape, 2) == 255, 0.0, 0.5)
    c = slice(1, 9)
    g1 = recip(
        (wx1[1:] + wx1[:-1]) + (wy1[c] + down(wy1[c], 1)) + (wz1[c] + down(wz1[c], 2))
    )

    arrive(r1_out)
    heard(2)
    tell(3)
    f1 = r1[...]
    d = g1 * f1[1:9] * C_FIRST
    q = f1[2:8] + planes_op(d, wx1[1:8], wy1[1:9], wz1[1:9], 1, 7)
    e = C_OLD * d[1:7] + C_NEW * (g1[1:7] * q)
    q = q[1:5] + planes_op(e, wx1[2:7], wy1[2:8], wz1[2:8], 1, 5)
    xp1[3:7, 8:16, :] = (d[2:6] + e[1:5])[:, 8:16, :]
    line = iota((24, 256), 0)
    inside = (line >= 4) & (line < 20)
    coarse1([tall(jnp.where(inside, q[2 * i] + q[2 * i + 1], 0.0)) for i in range(2)], r2)
    column(r2, 1)

    all_of(m2, 0).wait_recv()

    def to_flat(value):
        value = jnp.where(iota((16, 16, 128), 1) < 8, value, 0.0)
        wide = jnp.concatenate(
            [
                jnp.concatenate(
                    [value[4 * t] + value[4 * t + 1], value[4 * t + 2] + value[4 * t + 3]], axis=1
                )
                for t in range(4)
            ],
            axis=0,
        )
        wide = pick(wide, pair[...])
        tiles = [halve(thin, t, wide[16 * t : 16 * t + 16])[0][2:4] for t in range(4)]
        return jnp.concatenate(tiles, axis=1)

    v = b2[...]
    b3[32:34, :] = to_flat(v)
    heard(3)
    lines(b3, 2)
    shape = (16, 16, 128)
    edge = jnp.where(gy == GY - 1, 7, jnp.where(gy == 0, 3, -1))
    scale = 2.0 * 4.0**-2
    wx2 = harm(v, jnp.concatenate([v[1:], v[:1]])) * jnp.where(iota(shape, 0) == 15, 0.0, scale)
    wy2 = harm(v, up(v, 1)) * jnp.where(iota(shape, 1) == edge, 0.0, scale)
    wz2 = harm(v, up(v, 2)) * jnp.where(iota(shape, 2) == 127, 0.0, scale)
    g2 = recip(
        (wx2 + jnp.concatenate([wx2[-1:], wx2[:-1]]))
        + (wy2 + down(wy2, 1))
        + (wz2 + down(wz2, 2))
    )

    all_of(m2, 1).wait_recv()
    f2 = r2[...]
    d = g2 * f2 * C_FIRST
    q = f2 + ring_op(d, wx2, wy2, wz2)
    e = C_OLD * d + C_NEW * (g2 * q)
    q = q + ring_op(e, wx2, wy2, wz2)
    xp2[:, 4:8, :] = (d + e)[:, 4:8, :]
    rn2[:, 4:8, :] = f2[:, 4:8, :]
    q = jnp.where(iota((16, 16, 128), 1) >= 4, q, 0.0)
    r3[32:34, :] = to_flat(q)
    lines(r3, 3)
    xp2_out = [
        pltpu.make_async_remote_copy(
            ref.at[:, pl.ds(4, 4), :],
            ref.at[:, pl.ds(4 - 4 * b, 4), :],
            halo_s.at[6, 2 * j + k],
            halo_r.at[6, 2 * j + k],
            device_id=device((0, b)),
            device_id_type=MESH,
        )
        for j, ref in enumerate((xp2, rn2))
        for k, b in enumerate((-1, 1))
    ]
    start(xp2_out)
    start(xp1_out)
    start(xp0_out)

    all_of(m3, 2).wait_recv()
    v = b3[...]
    shape = (64, 512)
    scale = 2.0 * 4.0**-3
    lane = iota(shape, 1)
    edge = lax.rem(95 - 2 * gy, 64)
    wx3 = harm(v, up(v, 1, 64)) * jnp.where(lane >= 448, 0.0, scale)
    wy3 = harm(v, up(v, 0)) * jnp.where(iota(shape, 0) == edge, 0.0, scale)
    wz3 = harm(v, up(v, 1)) * jnp.where(lax.rem(lane, 64) == 63, 0.0, scale)
    g3 = recip((wx3 + down(wx3, 1, 64)) + (wy3 + down(wy3, 0)) + (wz3 + down(wz3, 1)))

    sent(b0_out + r0_out + b1_out + r1_out)
    all_of(m2, 0).wait_send()
    all_of(m2, 1).wait_send()
    all_of(m3, 2).wait_send()

    for c in fixed:
        c.wait()
    all_of(m3, 3).wait_recv()
    f3 = r3[...]
    d = g3 * f3 * C_FIRST
    q = f3 + flat_op(d, wx3, wy3, wz3)
    e = C_OLD * d + C_NEW * (g3 * q)
    q = q + flat_op(e, wx3, wy3, wz3)
    t = jnp.concatenate([q[:, 128 * t : 128 * t + 128] for t in range(4)], axis=0)
    t = dot(t, fwd[...])
    t = jnp.concatenate([t[64 * i : 64 * i + 64] for i in range(4)], axis=1)
    t = jnp.concatenate(cross_x(t, cross, 0), axis=1)
    t = dot(turn[:, 0:64], t) * table[...]
    t = dot(wind[:, 0:64], t)
    t = dot(jnp.concatenate(cross_x(t, cross, 1), axis=0), inv[...])
    t = jnp.concatenate([t[16 * i : 16 * i + 16] for i in range(4)], axis=1)
    w = slice(24, 40)
    x = d[w] + e[w] + t
    w3 = (wx3[w], wy3[w], wz3[w])
    q = f3[w] + flat_op(x, *w3)
    d = g3[w] * q * C_FIRST
    q = q + flat_op(d, *w3)
    x = x + d + (C_OLD * d + C_NEW * (g3[w] * q))

    wide = pick(
        jnp.concatenate([x[:, 128 * t : 128 * t + 128] for t in range(4)], axis=0), grow[...]
    )
    wide = [double(thin, 2 * t, wide[16 * t : 16 * t + 16], 4, 16, 16) for t in range(4)]
    wide = jnp.stack(
        [wide[i // 4][:, 128 * (i // 2 % 2) : 128 * (i // 2 % 2) + 128] for i in range(16)]
    )
    arrive(xp2_out)
    x = xp2[...] + wide
    q = rn2[...] + ring_op(x, wx2, wy2, wz2)
    d = g2 * q * C_FIRST
    q = q + ring_op(d, wx2, wy2, wz2)
    x = x + d + (C_OLD * d + C_NEW * (g2 * q))
    e2[2:18] = x
    e2[0:2] = x[14:16]
    e2[18:20] = x[0:2]

    wide = pick(jnp.concatenate([e2[2 * gx + i] for i in range(6)], axis=0), grow[...])
    wide = [double(thin, 2 * i, wide[16 * i : 16 * i + 16], 0, 0, 24) for i in range(6)]
    wide = jnp.stack([wide[(i + 1) // 2] for i in range(10)])
    arrive(xp1_out)
    x = xp1[...] + wide
    q = f1[1:9] + planes_op(x, wx1, wy1, wz1, 1, 9)
    d = g1 * q * C_FIRST
    q = q[1:7] + planes_op(d, wx1[1:8], wy1[1:9], wz1[1:9], 1, 7)
    x = x[2:8] + d[1:7] + (C_OLD * d[1:7] + C_NEW * (g1[1:7] * q))

    low = pick(jnp.concatenate([x[i, :, :128] for i in range(6)], axis=0), grow[...])
    high = pick(jnp.concatenate([x[i, :, 128:] for i in range(6)], axis=0), grow[...])
    wide = jnp.concatenate([low, high], axis=1)
    for i in range(6):
        y0[i] = double(thin, 4 * i, wide[24 * i : 24 * i + 24], 4, 16, 24)
    arrive(xp0_out)
    sent(xp0_out + xp1_out + xp2_out)
    all_of(m3, 3).wait_send()

    @pl.loop(1, 13, unroll=UNROLL)
    def _(i):
        e0[i] = xp0[i] + y0[(i + 3) // 2 - 2]

    @pl.loop(2, 12, unroll=UNROLL)
    def _(i):
        q = r0[i] + op0(e0, i)
        q0[i] = q
        d0[i] = g0[i] * q * C_FIRST

    @pl.loop(3, 11, unroll=UNROLL)
    def _(i):
        q = q0[i] + op0(d0, i)
        d = d0[i]
        x = e0[i] + d + (C_OLD * d + C_NEW * (g0[i] * q))
        ov[i - 3] = x[4:20]
        pltpu.make_async_copy(ov.at[i - 3], out.at[i - 3], done.at[i - 3]).start()

    for i in range(8):
        pltpu.make_async_copy(ov.at[i], out.at[i], done.at[i]).wait()


def local(right_side, inverse_density):
    consts = constants()
    far_spec = pl.BlockSpec(memory_space=pltpu.HBM)
    fine = pltpu.VMEM((14, 24, 512), F32)
    scratch = [pltpu.VMEM((8, 16, 512), F32)] * 3
    scratch += [pltpu.VMEM((6, 16, 512), F32), pltpu.VMEM((4, 16, 512), F32)]
    scratch += [fine] * 10 + [
        pltpu.VMEM((6, 24, 512), F32),
        pltpu.VMEM((24, 56, 128), F32),
        pltpu.VMEM((10, 24, 256), F32),
        pltpu.VMEM((10, 24, 256), F32),
        pltpu.VMEM((10, 24, 256), F32),
        pltpu.VMEM((16, 16, 128), F32),
        pltpu.VMEM((16, 16, 128), F32),
        pltpu.VMEM((16, 16, 128), F32),
        pltpu.VMEM((16, 16, 128), F32),
        pltpu.VMEM((20, 16, 128), F32),
        pltpu.VMEM((2 * len(COLUMN), 16, 128), F32),
        pltpu.VMEM((64, 512), F32),
        pltpu.VMEM((64, 512), F32),
        pltpu.VMEM((len(LINE), 8, 128), F32),
        pltpu.VMEM((128, 128), F32),
        pltpu.VMEM((128, 128), F32),
        pltpu.VMEM((64, 128), F32),
        pltpu.VMEM((16, 128), F32),
        pltpu.VMEM((64, 512), F32),
        pltpu.VMEM((64, 128), F32),
        pltpu.VMEM((256, 128), jnp.bfloat16),
        pltpu.VMEM((128, 256), jnp.bfloat16),
        pltpu.SemaphoreType.DMA((4, 4)),
        pltpu.SemaphoreType.DMA((7, 12)),
        pltpu.SemaphoreType.DMA((7, 12)),
        pltpu.SemaphoreType.DMA((4,)),
        pltpu.SemaphoreType.DMA((4,)),
        pltpu.SemaphoreType.REGULAR((4,)),
        pltpu.SemaphoreType.DMA((8,)),
    ]
    return pl.pallas_call(
        kernel,
        out_shape=jax.ShapeDtypeStruct((8, 16, 512), F32),
        in_specs=[far_spec] * 10,
        out_specs=far_spec,
        scratch_shapes=scratch,
        compiler_params=pltpu.CompilerParams(
            collective_id=0, has_side_effects=True, vmem_limit_bytes=63 * 2**20
        ),
    )(right_side, inverse_density, *consts)


def solution(mesh):
    return jax.shard_map(
        local,
        mesh=mesh,
        in_specs=(P("gx", "gy", None), P("gx", "gy", None)),
        out_specs=P("gx", "gy", None),
        check_vma=False,
    )
```

```python
import math
import numpy as np
import jax
import jax.numpy as jnp
from jax import lax
from jax.experimental import pallas as pl
from jax.experimental.pallas import tpu as pltpu
from jax.sharding import PartitionSpec as P

MESH = pl.DeviceIdType.MESH
F32 = jnp.float32
THETA = 1.25
DELTA = 0.75
SIGMA = THETA / DELTA
RHO0 = 1.0 / SIGMA
RHO1 = 1.0 / (2.0 * SIGMA - RHO0)
C_FIRST = 1.0 / THETA
C_OLD = RHO1 * RHO0
C_NEW = 2.0 * RHO1 / DELTA
GX, GY = 8, 32
UNROLL = True
NEIGHBOURS = [(1, 1), (1, -1), (-1, 1), (-1, -1), (0, 1), (0, -1), (1, 0), (-1, 0)]
COLUMN = [(a, 0) for a in (4, 5, 3, 6, 2, 7, 1)]


def hops(b):
    z = b % 8
    x = b // 8
    near = min(z, 8 - z) + min(x, 4 - x)
    x = (x + 1) % 4
    return near + min(z, 8 - z) + min(x, 4 - x) if z else 2 * near


LINE = sorted([(0, b) for b in range(1, GY)], key=lambda p: -hops(p[1]))
ROUNDS = [
    [(1, 0), (-1, 0), (0, 1), (0, -1)],
    [(2, 0), (-2, 0), (0, 2), (0, -2)],
    [(0, 4), (0, -4)],
    [(0, 8), (0, -8)],
]


def dct_matrix(count):
    wave = np.arange(count)[:, None].astype(np.float64)
    place = np.arange(count)[None, :].astype(np.float64)
    norms = np.where(wave == 0, math.sqrt(1.0 / count), math.sqrt(2.0 / count))
    return norms * np.cos(np.pi * wave * (2 * place + 1) / (2 * count))


def constants():
    cy, cz = dct_matrix(64), dct_matrix(64)
    along = np.kron(np.eye(2), cz.T)
    turned = np.stack([np.roll(cy, 32 - 2 * g, axis=1) for g in range(GY)])
    window = np.stack([np.pad(t.T[24:40], ((0, 0), (0, 64))) for t in turned])
    turned = np.pad(turned, ((0, 0), (0, 0), (0, 64)))
    lam = [2 - 2 * np.cos(np.pi * np.arange(n) / n) for n in (8, 64, 64)]
    total = (lam[1][:, None, None] + lam[0][None, :, None] + lam[2][None, None, :]) * 4.0**-3
    total[0, 0, 0] = 1.0
    table = 1.0 / total
    table[0, 0, 0] = 0.0
    pair = np.zeros((256, 128))
    pair[np.arange(256), np.arange(256) // 2] = 0.125
    grow = np.zeros((128, 256))
    grow[np.arange(256) // 2, np.arange(256)] = 1.0
    cx = dct_matrix(8)
    cross = np.zeros((2, 2, 4, 4, 128))
    for i in range(4):
        for j in range(4):
            for k, c in enumerate((cx, cx.T)):
                cross[k, 0, i, j] = np.repeat([c[2 * i, 2 * j], c[2 * i + 1, 2 * j + 1]], 64)
                cross[k, 1, i, j] = np.repeat([c[2 * i, 2 * j + 1], c[2 * i + 1, 2 * j]], 64)
    out = (along, along.T, turned, window, table.reshape(64, 512), cross.reshape(64, 128))
    out = tuple(np.ascontiguousarray(v, dtype=np.float32) for v in out)
    return out + (pair.astype(jnp.bfloat16), grow.astype(jnp.bfloat16))


def device(offset):
    gx, gy = lax.axis_index("gx"), lax.axis_index("gy")
    return (lax.rem(gx + (offset[0] % GX), GX), lax.rem(gy + (offset[1] % GY), GY))


def recip(value):
    guess = pl.reciprocal(value, approx=True)
    return guess * (2.0 - value * guess)


def harm(a, b):
    return (a * b) * recip(a + b)


def up(value, axis, step=1):
    return pltpu.roll(value, value.shape[axis] - step, axis)


def down(value, axis, step=1):
    return pltpu.roll(value, step, axis)


def parts(value):
    high = value.astype(jnp.bfloat16)
    return high, (value - high.astype(F32)).astype(jnp.bfloat16)


def pick(value, matrix):
    high, low = parts(value)
    return jnp.dot(high, matrix, preferred_element_type=F32) + jnp.dot(
        low, matrix, preferred_element_type=F32
    )


def halve(ref, base, value):
    tiles = []
    for t in range(value.shape[-1] // 128):
        ref[base + t, 0 : value.shape[0], :] = value[:, 128 * t : 128 * t + 128]
        count = value.shape[0] // 2
        tiles.append(
            ref[base + t, pl.ds(0, count, stride=2), :] + ref[base + t, pl.ds(1, count, stride=2), :]
        )
    return tiles


def double(ref, base, value, at, low, count):
    n = value.shape[0]
    tiles = []
    for t in range(value.shape[-1] // 128):
        v = value[:, 128 * t : 128 * t + 128]
        ref[base + t, pl.ds(at, n, stride=2), :] = v
        ref[base + t, pl.ds(at + 1, n, stride=2), :] = v
        tiles.append(ref[base + t, low : low + count, :])
    return jnp.concatenate(tiles, axis=1)


def cross_x(value, cross, k):
    v = [value[:, 128 * t : 128 * t + 128] for t in range(4)]
    w = [pltpu.roll(t, 64, 1) for t in v]
    out = []
    for i in range(4):
        acc = None
        for j in range(4):
            row = 32 * k + 4 * i + j
            term = v[j] * cross[row : row + 1, :] + w[j] * cross[row + 16 : row + 17, :]
            acc = term if acc is None else acc + term
        out.append(acc)
    return out


def dot(a, b):
    return jnp.dot(a, b, precision=lax.Precision.HIGHEST, preferred_element_type=F32)


def iota(shape, axis):
    return lax.broadcasted_iota(jnp.int32, shape, axis)


def halo_copies(ref, at, size, halo, corner, send, recv):
    copies = []
    for a, b in NEIGHBOURS:
        take, put = [], []
        for side, s0, n, h in zip((a, b), at, size, corner if a != 0 and b != 0 else halo):
            if side == 0:
                take.append((s0, n))
                put.append(s0)
            elif side > 0:
                take.append((s0 + n - h, h))
                put.append(s0 - h)
            else:
                take.append((s0, h))
                put.append(s0 + n)
        (x_from, x_count), (y_from, y_count) = take
        y_end = y_from + y_count
        ends = [y_from] + list(range(y_from // 8 * 8 + 8, y_end, 8)) + [y_end]
        for low, high in zip(ends[:-1], ends[1:]):
            k = len(copies)
            copies.append(
                pltpu.make_async_remote_copy(
                    ref.at[pl.ds(x_from, x_count), pl.ds(low, high - low), :],
                    ref.at[pl.ds(put[0], x_count), pl.ds(put[1] + low - y_from, high - low), :],
                    send.at[k],
                    recv.at[k],
                    device_id=device((a, b)),
                    device_id_type=MESH,
                )
            )
    return copies


def brick_copies(src, dst, side, halo, send, recv):
    copies = []
    for k, (a, b) in enumerate(NEIGHBOURS):
        h = halo - 1 if a != 0 and b != 0 else halo
        x = {0: pl.ds(0, 8), 1: pl.ds(8 - h, h), -1: pl.ds(0, h)}[a]
        y = {0: pl.ds(0, 16), 1: pl.ds(16 - h, h), -1: pl.ds(0, h)}[b]
        if b == 0:
            to = side.at[pl.ds(0 if a > 0 else h, h), :, :]
        else:
            put_x = {0: pl.ds(3, 8), 1: pl.ds(3 - h, h), -1: pl.ds(11, h)}[a]
            put_y = {1: pl.ds(4 - h, h), -1: pl.ds(20, h)}[b]
            to = dst.at[put_x, put_y, :]
        copies.append(
            pltpu.make_async_remote_copy(
                src.at[x, y, :],
                to,
                send.at[k],
                recv.at[k],
                device_id=device((a, b)),
                device_id_type=MESH,
            )
        )
    return copies


def start(copies):
    for c in copies:
        c.start()


def arrive(copies):
    for c in copies:
        c.wait_recv()


def sent(copies):
    for c in copies:
        c.wait_send()


def planes_op(v, wx, wy, wz, lo, hi):
    c = v[lo:hi]
    fx = wx[lo - 1 : hi] * (v[lo : hi + 1] - v[lo - 1 : hi])
    fy = wy[lo:hi] * (up(c, 1) - c)
    fz = wz[lo:hi] * (up(c, 2) - c)
    return (fx[1:] - fx[:-1]) + (fy - down(fy, 1)) + (fz - down(fz, 2))


def ring_op(v, wx, wy, wz):
    fx = wx * (jnp.concatenate([v[1:], v[:1]]) - v)
    fy = wy * (up(v, 1) - v)
    fz = wz * (up(v, 2) - v)
    fx = fx - jnp.concatenate([fx[-1:], fx[:-1]])
    return fx + (fy - down(fy, 1)) + (fz - down(fz, 2))


def flat_op(v, wx, wy, wz):
    fx = wx * (up(v, 1, 64) - v)
    fy = wy * (up(v, 0) - v)
    fz = wz * (up(v, 1) - v)
    return (fx - down(fx, 1, 64)) + (fy - down(fy, 0)) + (fz - down(fz, 1))


def kernel(
    r_in, b_in, fwd_in, inv_in, turn_in, wind_in, table_in, cross_in, pair_in, grow_in, out,
    ov, bs, rs, xb, xr, b0, r0, wx0, wy0, wz0, g0, d0, e0, q0, xp0, y0, thin,
    b1, r1, xp1, b2, r2, xp2, rn2, e2, m2, b3, r3, m3,
    fwd, inv, turn, wind, table, cross, pair, grow,
    local, halo_s, halo_r, many_s, many_r, near, done,
):
    gx, gy = lax.axis_index("gx"), lax.axis_index("gy")
    own = [
        pltpu.make_async_copy(b_in, bs, local.at[0, 0]),
        pltpu.make_async_copy(r_in, rs, local.at[0, 1]),
    ]
    small = [
        pltpu.make_async_copy(pair_in, pair, local.at[3, 2]),
        pltpu.make_async_copy(grow_in, grow, local.at[3, 3]),
    ]
    fixed = [
        pltpu.make_async_copy(fwd_in, fwd, local.at[2, 0]),
        pltpu.make_async_copy(inv_in, inv, local.at[2, 1]),
        pltpu.make_async_copy(turn_in.at[gy], turn, local.at[2, 2]),
        pltpu.make_async_copy(wind_in.at[gy], wind, local.at[2, 3]),
        pltpu.make_async_copy(table_in, table, local.at[3, 0]),
        pltpu.make_async_copy(cross_in, cross, local.at[3, 1]),
    ]
    barrier = pltpu.get_barrier_semaphore()
    for p in NEIGHBOURS:
        pl.semaphore_signal(barrier, inc=1, device_id=device(p), device_id_type=MESH)

    pl.semaphore_wait(barrier, len(NEIGHBOURS))

    def tell(k):
        for p in ROUNDS[k]:
            pl.semaphore_signal(near.at[k], inc=1, device_id=device(p), device_id_type=MESH)

    def heard(k):
        pl.semaphore_wait(near.at[k], len(ROUNDS[k]))

    b0_out = brick_copies(b_in, b0, xb, 3, halo_s.at[0], halo_r.at[0])
    r0_out = brick_copies(r_in, r0, xr, 2, halo_s.at[1], halo_r.at[1])
    b1_out = halo_copies(b1, (3, 8), (4, 8), (3, 8), (3, 8), halo_s.at[2], halo_r.at[2])
    r1_out = halo_copies(r1, (3, 8), (4, 8), (2, 6), (2, 5), halo_s.at[3], halo_r.at[3])
    xp0_out = halo_copies(xp0, (3, 4), (8, 16), (2, 2), (1, 1), halo_s.at[4], halo_r.at[4])
    xp1_out = halo_copies(xp1, (3, 8), (4, 8), (3, 3), (3, 3), halo_s.at[5], halo_r.at[5])
    start(b0_out + r0_out)
    tell(0)
    start(own + small + fixed)

    def column(ref, k):
        for a, _ in COLUMN:
            pltpu.make_async_remote_copy(
                ref.at[pl.ds(2 * gx, 2)],
                ref.at[pl.ds(2 * gx, 2)],
                many_s.at[k],
                many_r.at[k],
                device_id=device((a, 0)),
                device_id_type=MESH,
            ).start()

    def lines(ref, k):
        for _, b in LINE:
            pltpu.make_async_remote_copy(
                ref.at[pl.ds(32, 2), :],
                ref.at[pl.ds((32 - 2 * b) % 64, 2), :],
                many_s.at[k],
                many_r.at[k],
                device_id=device((0, b)),
                device_id_type=MESH,
            ).start()

    def all_of(ref, k):
        return pltpu.make_async_remote_copy(
            ref, ref, many_s.at[k], many_r.at[k], device_id=device((0, 1)), device_id_type=MESH
        )

    for c in small:
        c.wait()
    own[0].wait()

    @pl.loop(0, 8, unroll=True)
    def _(i):
        b0[i + 3, 4:20, :] = bs[i]

    def coarse0(planes, dst):
        tiles = [halve(thin, 4 * i, planes[i]) for i in range(4)]
        wide = [jnp.concatenate([tiles[i][t] for i in range(4)], axis=0) for t in range(4)]
        low = pick(jnp.concatenate(wide[:2], axis=1), pair[...])
        high = pick(jnp.concatenate(wide[2:], axis=1), pair[...])
        for i in range(4):
            dst[3 + i, 8:16, 0:128] = low[8 * i : 8 * i + 8]
            dst[3 + i, 8:16, 128:256] = high[8 * i : 8 * i + 8]
        return jnp.concatenate([low, high], axis=1)

    def coarse1(planes, dst):
        tiles = [halve(thin, 2 * i, planes[i]) for i in range(2)]
        wide = [jnp.concatenate([tiles[i][t] for i in range(2)], axis=0) for t in range(2)]
        low = pick(jnp.concatenate(wide, axis=1), pair[...])
        for i in range(2):
            dst[2 * gx + i] = low[16 * i : 16 * i + 16]

    coarse0([bs[2 * i] + bs[2 * i + 1] for i in range(4)], b1)
    start(b1_out)
    own[1].wait()

    @pl.loop(0, 8, unroll=True)
    def _(i):
        r0[i + 3, 4:20, :] = rs[i]

    arrive(b0_out)
    for i in range(3):
        b0[i, 4:20, :] = xb[i]
        b0[11 + i, 4:20, :] = xb[3 + i]

    row = iota((24, 512), 0)
    lane = iota((24, 512), 1)
    edge = jnp.where(gy == GY - 1, 19, jnp.where(gy == 0, 3, -1))
    mul_y = jnp.where(row == edge, 0.0, 2.0)
    mul_z = jnp.where(lane == 511, 0.0, 2.0)
    cut0 = jnp.where(gx == GX - 1, 10, jnp.where(gx == 0, 2, -1))

    wx0[0] = 2.0 * harm(b0[0], b0[1])

    @pl.loop(1, 13, unroll=UNROLL)
    def _(i):
        c = b0[i]
        wx = harm(c, b0[i + 1]) * jnp.where(i == cut0, 0.0, 2.0)
        wy = harm(c, up(c, 0)) * mul_y
        wz = harm(c, up(c, 1)) * mul_z
        wx0[i] = wx
        wy0[i] = wy
        wz0[i] = wz
        g = recip((wx + wx0[i - 1]) + (wy + down(wy, 0)) + (wz + down(wz, 1)))
        g0[i] = g

    arrive(r0_out)
    heard(0)
    tell(1)
    for i in range(2):
        r0[1 + i, 4:20, :] = xr[i]
        r0[11 + i, 4:20, :] = xr[2 + i]

    @pl.loop(1, 13, unroll=UNROLL)
    def _(i):
        d0[i] = g0[i] * r0[i] * C_FIRST

    def op0(ref, i):
        c = ref[i]
        fy = wy0[i] * (up(c, 0) - c)
        fz = wz0[i] * (up(c, 1) - c)
        fx = wx0[i] * (ref[i + 1] - c) - wx0[i - 1] * (c - ref[i - 1])
        return fx + (fy - down(fy, 0)) + (fz - down(fz, 1))

    @pl.loop(2, 12, unroll=UNROLL)
    def _(i):
        q = r0[i] + op0(d0, i)
        q0[i] = q
        e0[i] = C_OLD * d0[i] + C_NEW * (g0[i] * q)

    @pl.loop(3, 11, unroll=UNROLL)
    def _(i):
        q = q0[i] + op0(e0, i)
        q0[i] = q
        x = d0[i] + e0[i]
        xp0[i, 4:20, :] = x[4:20]

    coarse0([(q0[3 + 2 * i] + q0[4 + 2 * i])[4:20] for i in range(4)], r1)
    start(r1_out)
    heard(1)
    tell(2)

    arrive(b1_out)
    v = b1[...]
    blank = jnp.zeros((8, 256), F32)

    def tall(value):
        return jnp.concatenate([value, blank], axis=0)

    coarse1([tall(v[3 + 2 * i] + v[4 + 2 * i]) for i in range(2)], b2)
    column(b2, 0)
    shape = (10, 24, 256)
    edge = jnp.where(gy == GY - 1, 15, jnp.where(gy == 0, 7, -1))
    cut = jnp.where(gx == GX - 1, 6, jnp.where(gx == 0, 2, -1))
    keep_x = jnp.where(iota((9, 24, 256), 0) == cut, 0.0, 0.5)
    wx1 = harm(v[:-1], v[1:]) * keep_x
    wy1 = harm(v, up(v, 1)) * jnp.where(iota(shape, 1) == edge, 0.0, 0.5)
    wz1 = harm(v, up(v, 2)) * jnp.where(iota(shape, 2) == 255, 0.0, 0.5)
    c = slice(1, 9)
    g1 = recip(
        (wx1[1:] + wx1[:-1]) + (wy1[c] + down(wy1[c], 1)) + (wz1[c] + down(wz1[c], 2))
    )

    arrive(r1_out)
    heard(2)
    tell(3)
    f1 = r1[...]
    d = g1 * f1[1:9] * C_FIRST
    q = f1[2:8] + planes_op(d, wx1[1:8], wy1[1:9], wz1[1:9], 1, 7)
    e = C_OLD * d[1:7] + C_NEW * (g1[1:7] * q)
    q = q[1:5] + planes_op(e, wx1[2:7], wy1[2:8], wz1[2:8], 1, 5)
    xp1[3:7, 8:16, :] = (d[2:6] + e[1:5])[:, 8:16, :]
    line = iota((24, 256), 0)
    inside = (line >= 4) & (line < 20)
    coarse1([tall(jnp.where(inside, q[2 * i] + q[2 * i + 1], 0.0)) for i in range(2)], r2)
    column(r2, 1)

    all_of(m2, 0).wait_recv()

    def to_flat(value):
        value = jnp.where(iota((16, 16, 128), 1) < 8, value, 0.0)
        wide = jnp.concatenate(
            [
                jnp.concatenate(
                    [value[4 * t] + value[4 * t + 1], value[4 * t + 2] + value[4 * t + 3]], axis=1
                )
                for t in range(4)
            ],
            axis=0,
        )
        wide = pick(wide, pair[...])
        tiles = [halve(thin, t, wide[16 * t : 16 * t + 16])[0][2:4] for t in range(4)]
        return jnp.concatenate(tiles, axis=1)

    v = b2[...]
    b3[32:34, :] = to_flat(v)
    heard(3)
    lines(b3, 2)
    shape = (16, 16, 128)
    edge = jnp.where(gy == GY - 1, 7, jnp.where(gy == 0, 3, -1))
    scale = 2.0 * 4.0**-2
    wx2 = harm(v, jnp.concatenate([v[1:], v[:1]])) * jnp.where(iota(shape, 0) == 15, 0.0, scale)
    wy2 = harm(v, up(v, 1)) * jnp.where(iota(shape, 1) == edge, 0.0, scale)
    wz2 = harm(v, up(v, 2)) * jnp.where(iota(shape, 2) == 127, 0.0, scale)
    g2 = recip(
        (wx2 + jnp.concatenate([wx2[-1:], wx2[:-1]]))
        + (wy2 + down(wy2, 1))
        + (wz2 + down(wz2, 2))
    )

    all_of(m2, 1).wait_recv()
    f2 = r2[...]
    d = g2 * f2 * C_FIRST
    q = f2 + ring_op(d, wx2, wy2, wz2)
    e = C_OLD * d + C_NEW * (g2 * q)
    q = q + ring_op(e, wx2, wy2, wz2)
    xp2[:, 4:8, :] = (d + e)[:, 4:8, :]
    rn2[:, 4:8, :] = f2[:, 4:8, :]
    q = jnp.where(iota((16, 16, 128), 1) >= 4, q, 0.0)
    r3[32:34, :] = to_flat(q)
    lines(r3, 3)
    xp2_out = [
        pltpu.make_async_remote_copy(
            ref.at[:, pl.ds(4, 4), :],
            ref.at[:, pl.ds(4 - 4 * b, 4), :],
            halo_s.at[6, 2 * j + k],
            halo_r.at[6, 2 * j + k],
            device_id=device((0, b)),
            device_id_type=MESH,
        )
        for j, ref in enumerate((xp2, rn2))
        for k, b in enumerate((-1, 1))
    ]
    start(xp2_out)
    start(xp1_out)
    start(xp0_out)

    all_of(m3, 2).wait_recv()
    v = b3[...]
    shape = (64, 512)
    scale = 2.0 * 4.0**-3
    lane = iota(shape, 1)
    edge = lax.rem(95 - 2 * gy, 64)
    wx3 = harm(v, up(v, 1, 64)) * jnp.where(lane >= 448, 0.0, scale)
    wy3 = harm(v, up(v, 0)) * jnp.where(iota(shape, 0) == edge, 0.0, scale)
    wz3 = harm(v, up(v, 1)) * jnp.where(lax.rem(lane, 64) == 63, 0.0, scale)
    g3 = recip((wx3 + down(wx3, 1, 64)) + (wy3 + down(wy3, 0)) + (wz3 + down(wz3, 1)))

    sent(b0_out + r0_out + b1_out + r1_out)
    all_of(m2, 0).wait_send()
    all_of(m2, 1).wait_send()
    all_of(m3, 2).wait_send()

    for c in fixed:
        c.wait()
    all_of(m3, 3).wait_recv()
    f3 = r3[...]
    d = g3 * f3 * C_FIRST
    q = f3 + flat_op(d, wx3, wy3, wz3)
    e = C_OLD * d + C_NEW * (g3 * q)
    q = q + flat_op(e, wx3, wy3, wz3)
    t = jnp.concatenate([q[:, 128 * t : 128 * t + 128] for t in range(4)], axis=0)
    t = dot(t, fwd[...])
    t = jnp.concatenate([t[64 * i : 64 * i + 64] for i in range(4)], axis=1)
    t = jnp.concatenate(cross_x(t, cross, 0), axis=1)
    t = dot(turn[:, 0:64], t) * table[...]
    t = dot(wind[:, 0:64], t)
    t = dot(jnp.concatenate(cross_x(t, cross, 1), axis=0), inv[...])
    t = jnp.concatenate([t[16 * i : 16 * i + 16] for i in range(4)], axis=1)
    w = slice(24, 40)
    x = d[w] + e[w] + t
    w3 = (wx3[w], wy3[w], wz3[w])
    q = f3[w] + flat_op(x, *w3)
    d = g3[w] * q * C_FIRST
    q = q + flat_op(d, *w3)
    x = x + d + (C_OLD * d + C_NEW * (g3[w] * q))

    wide = pick(
        jnp.concatenate([x[:, 128 * t : 128 * t + 128] for t in range(4)], axis=0), grow[...]
    )
    wide = [double(thin, 2 * t, wide[16 * t : 16 * t + 16], 4, 16, 16) for t in range(4)]
    wide = jnp.stack(
        [wide[i // 4][:, 128 * (i // 2 % 2) : 128 * (i // 2 % 2) + 128] for i in range(16)]
    )
    arrive(xp2_out)
    x = xp2[...] + wide
    q = rn2[...] + ring_op(x, wx2, wy2, wz2)
    d = g2 * q * C_FIRST
    q = q + ring_op(d, wx2, wy2, wz2)
    x = x + d + (C_OLD * d + C_NEW * (g2 * q))
    e2[2:18] = x
    e2[0:2] = x[14:16]
    e2[18:20] = x[0:2]

    wide = pick(jnp.concatenate([e2[2 * gx + i] for i in range(6)], axis=0), grow[...])
    wide = [double(thin, 2 * i, wide[16 * i : 16 * i + 16], 0, 0, 24) for i in range(6)]
    wide = jnp.stack([wide[(i + 1) // 2] for i in range(10)])
    arrive(xp1_out)
    x = xp1[...] + wide
    q = f1[1:9] + planes_op(x, wx1, wy1, wz1, 1, 9)
    d = g1 * q * C_FIRST
    q = q[1:7] + planes_op(d, wx1[1:8], wy1[1:9], wz1[1:9], 1, 7)
    x = x[2:8] + d[1:7] + (C_OLD * d[1:7] + C_NEW * (g1[1:7] * q))

    low = pick(jnp.concatenate([x[i, :, :128] for i in range(6)], axis=0), grow[...])
    high = pick(jnp.concatenate([x[i, :, 128:] for i in range(6)], axis=0), grow[...])
    wide = jnp.concatenate([low, high], axis=1)
    for i in range(6):
        y0[i] = double(thin, 4 * i, wide[24 * i : 24 * i + 24], 4, 16, 24)
    arrive(xp0_out)

    @pl.loop(1, 13, unroll=UNROLL)
    def _(i):
        e0[i] = xp0[i] + y0[(i + 3) // 2 - 2]

    @pl.loop(2, 12, unroll=UNROLL)
    def _(i):
        q = r0[i] + op0(e0, i)
        q0[i] = q
        d0[i] = g0[i] * q * C_FIRST

    @pl.loop(3, 11, unroll=UNROLL)
    def _(i):
        q = q0[i] + op0(d0, i)
        d = d0[i]
        x = e0[i] + d + (C_OLD * d + C_NEW * (g0[i] * q))
        ov[i - 3] = x[4:20]
        pltpu.make_async_copy(ov.at[i - 3], out.at[i - 3], done.at[i - 3]).start()

    sent(xp0_out + xp1_out + xp2_out)
    all_of(m3, 3).wait_send()
    for i in range(8):
        pltpu.make_async_copy(ov.at[i], out.at[i], done.at[i]).wait()


def local(right_side, inverse_density):
    consts = constants()
    far_spec = pl.BlockSpec(memory_space=pltpu.HBM)
    fine = pltpu.VMEM((14, 24, 512), F32)
    scratch = [pltpu.VMEM((8, 16, 512), F32)] * 3
    scratch += [pltpu.VMEM((6, 16, 512), F32), pltpu.VMEM((4, 16, 512), F32)]
    scratch += [fine] * 10 + [
        pltpu.VMEM((6, 24, 512), F32),
        pltpu.VMEM((24, 56, 128), F32),
        pltpu.VMEM((10, 24, 256), F32),
        pltpu.VMEM((10, 24, 256), F32),
        pltpu.VMEM((10, 24, 256), F32),
        pltpu.VMEM((16, 16, 128), F32),
        pltpu.VMEM((16, 16, 128), F32),
        pltpu.VMEM((16, 16, 128), F32),
        pltpu.VMEM((16, 16, 128), F32),
        pltpu.VMEM((20, 16, 128), F32),
        pltpu.VMEM((2 * len(COLUMN), 16, 128), F32),
        pltpu.VMEM((64, 512), F32),
        pltpu.VMEM((64, 512), F32),
        pltpu.VMEM((len(LINE), 8, 128), F32),
        pltpu.VMEM((128, 128), F32),
        pltpu.VMEM((128, 128), F32),
        pltpu.VMEM((64, 128), F32),
        pltpu.VMEM((16, 128), F32),
        pltpu.VMEM((64, 512), F32),
        pltpu.VMEM((64, 128), F32),
        pltpu.VMEM((256, 128), jnp.bfloat16),
        pltpu.VMEM((128, 256), jnp.bfloat16),
        pltpu.SemaphoreType.DMA((4, 4)),
        pltpu.SemaphoreType.DMA((7, 12)),
        pltpu.SemaphoreType.DMA((7, 12)),
        pltpu.SemaphoreType.DMA((4,)),
        pltpu.SemaphoreType.DMA((4,)),
        pltpu.SemaphoreType.REGULAR((4,)),
        pltpu.SemaphoreType.DMA((8,)),
    ]
    return pl.pallas_call(
        kernel,
        out_shape=jax.ShapeDtypeStruct((8, 16, 512), F32),
        in_specs=[far_spec] * 10,
        out_specs=far_spec,
        scratch_shapes=scratch,
        compiler_params=pltpu.CompilerParams(
            collective_id=0, has_side_effects=True, vmem_limit_bytes=63 * 2**20
        ),
    )(right_side, inverse_density, *consts)


def solution(mesh):
    return jax.shard_map(
        local,
        mesh=mesh,
        in_specs=(P("gx", "gy", None), P("gx", "gy", None)),
        out_specs=P("gx", "gy", None),
        check_vma=False,
    )
```
